128 devices in a mesh: gx: 8 (over y, core), gy: 16 (over z, x).
Axes of the slice: x: 4, y: 4, z: 4, core: 2. Of those that a mesh axis runs over, the one named last changes fastest.
Arguments:
- embeddings: bfloat16 [1024, 128, 1024], P(('gx', 'gy')), may hold values from -120 to 120
- block_cluster: int32 [1024], P(('gx', 'gy')), may hold values from 0 to 1023, as said below
- block_rows: int32 [1024], P(('gx', 'gy')), may hold values from 1 to 128
Outputs:
- best: float32 [1024, 128], P(('gx', 'gy'))
The draws below stay inside these ranges and needn't reach their ends.
Inputs may be any that keep to these rules, and one draw needn't show every extreme that they name: `block_cluster`: ids never fall along the blocks, so the blocks of one cluster are consecutive; one cluster holds at most 57 blocks, and some cluster holds exactly 57.
All inputs are finite; a program needn't handle non-finite values.
Results may differ from the reference program's by a relative error of at most 0.00055.
Values may be sent and summed in bfloat16 or wider, within the bound.
No kernel may reach another device: no remote copies, remote signals or barrier semaphores. Data moves between devices by JAX's collectives and lax.ppermute only.
A program may use at most 128 MiB of HBM per device.

```python
import jax
import jax.numpy as jnp
from jax import lax

D = 1024
BR = 128
BLK_DEV = 8
SPAN = 57
BLOCKS = 1024


def layout(key):
    first_key, second_key = jax.random.split(key)
    blocks = jnp.arange(BLOCKS, dtype=jnp.int32)
    anchor = BLK_DEV - 1 + BLK_DEV * jax.random.randint(first_key, (), 0, 2)
    relative = blocks - anchor
    window = jnp.where(relative >= 0, relative // SPAN, 0)
    opening = (relative >= 0) & (relative % SPAN == 0)
    window_start = anchor + window * SPAN
    whole = (relative >= 0) & (window_start % BLK_DEV == BLK_DEV - 1)
    coin = jax.random.randint(second_key, (BLOCKS,), 0, 3) == 0
    cut_here = (opening | coin & jnp.logical_not(whole)) & (blocks > 0)
    counted = jnp.cumsum(cut_here.astype(jnp.int32)).astype(jnp.int32)
    ident = jnp.where(counted == counted[BLOCKS - 1], BLOCKS - 1, counted).astype(jnp.int32)
    begins = cut_here | (blocks == 0)
    cluster_start = lax.cummax(jnp.where(begins, blocks, 0), axis=0)
    next_cut = jnp.concatenate([cut_here[1:], jnp.ones((1,), bool)], axis=0)
    cluster_end = lax.cummin(jnp.where(next_cut, blocks, BLOCKS), axis=0, reverse=True)
    return (ident, cluster_start, cluster_end - cluster_start + 1)


def draw_block_cluster(key, part):
    ident, cluster_start, cluster_size = layout(key)
    return ident


def draw_block_rows(key, part):
    key = jax.random.fold_in(key, 7)
    first_key, second_key = jax.random.split(key)
    filled = jax.random.randint(first_key, (BLOCKS,), 0, 10) < 7
    counted = jax.random.randint(second_key, (BLOCKS,), 1, BR)
    result = jnp.where(filled, BR, counted).astype(jnp.int32)
    return result.at[0].set(BR)


def draw_embeddings(key, part):
    ident, cluster_start, cluster_size = layout(key)
    key = jax.random.fold_in(key, 5)
    keys = jax.random.split(key, 5)
    noise = jax.random.normal(keys[0], (BLOCKS, BR, D), jnp.float32)
    partner_block = cluster_start[:, None] + jax.random.randint(keys[1], (BLOCKS, BR), 0, 1 << 20) % cluster_size[:, None]
    partner_row = jax.random.randint(keys[2], (BLOCKS, BR), 0, BR)
    mixing = jax.random.uniform(keys[3], (BLOCKS, BR, 1), jnp.float32, 0.35, 0.95)
    centres = jax.random.normal(keys[4], (BLOCKS, D), jnp.float32)
    values = mixing * noise[partner_block, partner_row] + (1.0 - mixing) * noise + 0.4 * centres[ident][:, None, :]
    return jnp.clip(values, -120.0, 120.0).astype(jnp.bfloat16)


def setup_inputs(seed: int = 0) -> dict:
    arg_keys = jax.random.split(jax.random.key(seed), 4)
    return {
        "embeddings": draw_embeddings(jax.random.fold_in(arg_keys[3], 71), 0),
        "block_cluster": draw_block_cluster(jax.random.fold_in(arg_keys[3], 71), 0),
        "block_rows": draw_block_rows(jax.random.fold_in(arg_keys[3], 71), 0),
    }


epsilon = 1e-06

def normalize(embeddings):
    values = embeddings.astype(jnp.float32)
    factor = lax.rsqrt(lax.optimization_barrier(jnp.sum(values * values, axis=-1, keepdims=True)) + epsilon)
    return (values * factor).astype(jnp.bfloat16)

def reference(embeddings, block_cluster, block_rows):
    units = normalize(embeddings).astype(jnp.float32)
    position = lax.broadcasted_iota(jnp.int32, (BLOCKS, BR), 1)
    valid = position < block_rows[:, None]
    padded_units = jnp.concatenate([units, jnp.zeros((SPAN, BR, D), jnp.float32)], axis=0)
    padded_cluster = jnp.concatenate([block_cluster, jnp.full((SPAN,), -1, jnp.int32)], axis=0)
    padded_valid = jnp.concatenate([valid, jnp.zeros((SPAN, BR), bool)], axis=0)
    same_row = lax.broadcasted_iota(jnp.int32, (BR, BR), 0) == lax.broadcasted_iota(jnp.int32, (BR, BR), 1)

    def step(current, offset):
        other_units = lax.dynamic_slice_in_dim(padded_units, offset, BLOCKS, 0)
        other_cluster = lax.dynamic_slice_in_dim(padded_cluster, offset, BLOCKS, 0)
        other_valid = lax.dynamic_slice_in_dim(padded_valid, offset, BLOCKS, 0)
        similar = jnp.einsum('aid,ajd->aij', units, other_units, precision=lax.Precision.HIGHEST)
        allowed = (block_cluster == other_cluster)[:, None, None] & valid[:, :, None] & other_valid[:, None, :]
        allowed = allowed & ((offset > 0) | jnp.logical_not(same_row))[None, :, :]
        levels = jnp.where(allowed, similar + 1.0, 0.0)
        current = jnp.maximum(current, lax.optimization_barrier(jnp.max(levels, axis=2)))
        columns = lax.optimization_barrier(jnp.max(levels, axis=1))
        padded_columns = jnp.concatenate([jnp.zeros((SPAN, BR), jnp.float32), columns], axis=0)
        current = jnp.maximum(current, lax.dynamic_slice_in_dim(padded_columns, SPAN - offset, BLOCKS, 0))
        return (current, None)
    current, _ = lax.scan(step, jnp.zeros((BLOCKS, BR), jnp.float32), jnp.arange(SPAN, dtype=jnp.int32))
    return jnp.where(valid, current - 1.0, 0.0)
```

```python
import functools

import jax
import jax.numpy as jnp
from jax import lax
from jax.experimental import pallas as pl
from jax.experimental.pallas import tpu as pltpu
from jax.sharding import PartitionSpec as P

AXES = ("gx", "gy")
ROW = 4
LOW = -4.0
EPSILON = 1e-06
VMEM = 40 * 1024 * 1024

OWN, NEXT, PREV, UP, DOWN, UP_NEXT, DOWN_PREV = range(0, 56, 8)
ONE, LEFT_HALF, EVEN, ODD, EVEN_FIRST, ODD_LAST = range(56, 62)


def shifted(array, pairs):
    return lax.ppermute(array, AXES, pairs)


def smem():
    return pl.BlockSpec(memory_space=pltpu.SMEM)


def vmem():
    return pl.BlockSpec(memory_space=pltpu.VMEM)


def unit_kernel(live, embeddings, units):
    blocks, count, _ = embeddings.shape
    position = lax.broadcasted_iota(jnp.int32, (count, 1), 0)

    def normalize(b, carry):
        values = embeddings[b].astype(jnp.float32)
        factor = lax.rsqrt(jnp.sum(values * values, axis=-1, keepdims=True) + EPSILON)
        unit = values * factor
        units[b] = jnp.where(position < live[b], unit, unit[0:1]).astype(jnp.bfloat16)
        return carry

    lax.fori_loop(0, blocks, normalize, 0)


def normalize(embeddings, live):
    return pl.pallas_call(
        unit_kernel,
        out_shape=jax.ShapeDtypeStruct(embeddings.shape, jnp.bfloat16),
        in_specs=[smem(), vmem()],
        out_specs=vmem(),
        compiler_params=pltpu.CompilerParams(vmem_limit_bytes=VMEM),
        cost_estimate=pl.CostEstimate(flops=4 * embeddings.size, bytes_accessed=4 * embeddings.size, transcendentals=0),
    )(live, embeddings)


def own_kernel(cluster, live, units, best):
    blocks, count, width = units.shape
    rows = lax.broadcasted_iota(jnp.int32, (count, count), 0)
    columns = lax.broadcasted_iota(jnp.int32, (count, count), 1)
    other = units[...].reshape(blocks * count, width)

    def chunk(i, carry):
        similar = lax.dot_general(
            units[pl.ds(2 * i, 2)].reshape(2 * count, width), other,
            (((1,), (1,)), ((), ())), preferred_element_type=jnp.float32,
        )
        for k in range(2):
            a = 2 * i + k
            top = None
            for j in range(blocks):
                part = similar[k * count:(k + 1) * count, j * count:(j + 1) * count]
                part = part + jnp.where(cluster[a] == cluster[j], 0.0, LOW)
                hidden = (a == j) & ((rows == columns) | (columns >= live[j]))
                part = jnp.where(hidden, LOW, part)
                top = part if top is None else jnp.maximum(top, part)
            best[pl.ds(a, 1)] = jnp.max(top.T, axis=0, keepdims=True)
        return carry

    lax.fori_loop(0, blocks // 2, chunk, 0)


def own_tile(units, cluster, live):
    blocks, count, width = units.shape
    return pl.pallas_call(
        own_kernel,
        out_shape=jax.ShapeDtypeStruct((blocks, count), jnp.float32),
        in_specs=[smem(), smem(), vmem()],
        out_specs=vmem(),
        compiler_params=pltpu.CompilerParams(vmem_limit_bytes=VMEM),
        cost_estimate=pl.CostEstimate(
            flops=2 * (blocks * count) ** 2 * width, bytes_accessed=2 * blocks * count * width, transcendentals=0
        ),
    )(cluster, live, units)


def pairs_kernel(parts, jobs, items, ids, *refs):
    arrays, outs = refs[:len(parts)], refs[len(parts):]
    for out in outs:
        out[...] = jnp.full(out.shape, LOW, jnp.float32)
    for first, second, flag in jobs:
        a, b = arrays[first], arrays[second]
        a_item, a_base, a_offset = parts[first]
        b_item, b_base, b_offset = parts[second]
        a_out, b_out = outs[items.index(a_item)], outs[items.index(b_item)]
        count, width = a.shape[1], a.shape[2]
        b_blocks = b.shape[0]

        @pl.when(ids[flag] > 0)
        def _(a=a, b=b, a_out=a_out, b_out=b_out, a_base=a_base, b_base=b_base,
              a_offset=a_offset, b_offset=b_offset, b_blocks=b_blocks):
            a0 = a_base + a_offset
            b0 = b_base + b_offset
            least, most = ids[b0], ids[b0 + b_blocks - 1]

            def chunk(i, carry):
                meets = (ids[a0 + 2 * i + 1] >= least) & (ids[a0 + 2 * i] <= most)

                @pl.when(meets)
                def _():
                    similar = lax.dot_general(
                        a[pl.ds(2 * i, 2)].reshape(2 * count, width),
                        b[...].reshape(b_blocks * count, width),
                        (((1,), (1,)), ((), ())), preferred_element_type=jnp.float32,
                    )
                    tops = [None, None]
                    for j in range(b_blocks):
                        column = None
                        for k in range(2):
                            part = similar[k * count:(k + 1) * count, j * count:(j + 1) * count]
                            part = part + jnp.where(ids[a0 + 2 * i + k] == ids[b0 + j], 0.0, LOW)
                            tops[k] = part if tops[k] is None else jnp.maximum(tops[k], part)
                            column = part if column is None else jnp.maximum(column, part)
                        here = pl.ds(b_offset + j, 1)
                        b_out[here] = jnp.maximum(b_out[here], jnp.max(column, axis=0, keepdims=True))
                    for k in range(2):
                        here = pl.ds(a_offset + 2 * i + k, 1)
                        a_out[here] = jnp.maximum(a_out[here], jnp.max(tops[k].T, axis=0, keepdims=True))

                return carry

            lax.fori_loop(0, a.shape[0] // 2, chunk, 0)


def compare(ids, parts, jobs):
    items = []
    for _, item, _, _ in parts:
        if item not in items:
            items.append(item)
    arrays = [part[0] for part in parts]
    blocks = 8
    count, width = arrays[0].shape[1], arrays[0].shape[2]
    flops = sum(2 * arrays[f].shape[0] * arrays[s].shape[0] * count * count * width for f, s, _ in jobs)
    found = pl.pallas_call(
        functools.partial(pairs_kernel, [part[1:] for part in parts], jobs, items),
        out_shape=[jax.ShapeDtypeStruct((blocks, count), jnp.float32) for _ in items],
        in_specs=[smem()] + [vmem() for _ in arrays],
        out_specs=[vmem() for _ in items],
        compiler_params=pltpu.CompilerParams(vmem_limit_bytes=VMEM),
        cost_estimate=pl.CostEstimate(
            flops=flops, bytes_accessed=sum(2 * a.size for a in arrays), transcendentals=0
        ),
    )(ids, *arrays)
    return dict(zip(items, found))


def merged(*results):
    total = {}
    for result in results:
        for item, value in result.items():
            total[item] = jnp.maximum(total[item], value) if item in total else value
    return total


def ring(devices, by, rows=None):
    return [
        (row * ROW + x, row * ROW + (x + by) % ROW)
        for row in range(devices // ROW) if rows is None or rows(row) for x in range(ROW)
    ]


def column(devices, by, rows=None):
    return [
        (i, i + by * ROW) for i in range(devices)
        if 0 <= i + by * ROW < devices and (rows is None or rows((i + by * ROW) // ROW))
    ]


def body(embeddings, block_cluster, block_rows):
    minor = lax.axis_size(AXES[1])
    devices = lax.axis_size(AXES[0]) * minor
    blocks, count, _ = embeddings.shape
    major = lax.axis_index(AXES[0])
    me = lax.axis_index(AXES).astype(jnp.int32)
    x, row = me % ROW, me // ROW
    last_row = devices // ROW - 1
    even_site = major % 2 == 0

    def even(r):
        return (r * ROW // minor) % 2 == 0

    def odd(r):
        return not even(r)

    right, left = ring(devices, 1), ring(devices, -1)
    below, above = column(devices, 1), column(devices, -1)

    line = jnp.stack([
        block_cluster, shifted(block_cluster, left), shifted(block_cluster, ring(devices, 2)), shifted(block_cluster, right)
    ])
    line_up = jnp.where(row > 0, shifted(line, below), -1)
    line_down = jnp.where(row < last_row, shifted(line, above), -2)
    down_prev = jnp.where(even_site & (x == 0), line_up[3], jnp.where(~even_site & (x == ROW - 1), line_down[1], line_down[3]))
    flags = jnp.stack([
        x >= 0, x < 2, even_site, ~even_site, even_site & (x == 0), ~even_site & (x == ROW - 1), x < 0, x < 0
    ]).astype(jnp.int32)
    ids = jnp.concatenate([line[0], line[1], line[3], line_up[0], line_down[0], line_up[1], down_prev, flags])

    units = normalize(embeddings, block_rows)
    to_down, to_up = shifted(units, below), shifted(units, above)
    nxt, prv = shifted(units, left), shifted(units, right)
    up, down = to_down, to_up
    up_next_even = shifted(up, ring(devices, -1, even))
    down_prev_even = shifted(jnp.where(x == ROW - 1, up, down), ring(devices, 1, even))
    up_next_odd = shifted(nxt, column(devices, 1, odd))
    down_prev_odd = shifted(jnp.where(x == ROW - 1, nxt, prv), column(devices, -1, odd))

    best = own_tile(units, block_cluster, block_rows)
    first = compare(
        ids, [(units, "own", OWN, 0), (nxt, "next", NEXT, 0), (prv, "prev", PREV, 0), (up, "up", UP, 0)],
        [(0, 1, ONE), (1, 2, LEFT_HALF), (0, 3, ONE), (1, 3, ONE), (2, 3, ONE)],
    )
    second = compare(
        ids,
        [
            (prv, "prev", PREV, 0), (up, "up", UP, 0), (down, "down", DOWN, 0),
            (up_next_even, "up_next", UP_NEXT, 0), (down_prev_even, "down_prev", DOWN_PREV, 0),
            (up_next_odd, "up_next", UP_NEXT, 0), (down_prev_odd, "down_prev", DOWN_PREV, 0),
        ],
        [
            (0, 3, EVEN), (2, 3, EVEN), (3, 4, EVEN), (2, 4, EVEN_FIRST),
            (0, 5, ODD), (2, 5, ODD), (5, 6, ODD), (1, 6, ODD_LAST),
        ],
    )
    found = merged(first, second)
    none = jnp.full((blocks, count), LOW, jnp.float32)
    early, late = even_site & (x == 0), ~even_site & (x == ROW - 1)
    from_prev = shifted(
        jnp.stack([found["next"], found["up_next"], jnp.where(late, found["down_prev"], none)]), right
    )
    from_next = shifted(
        jnp.stack([
            found["prev"], jnp.where(early, found["down_prev"], none),
            jnp.where(early | late, none, found["down_prev"]),
        ]), left
    )
    around = jnp.maximum(from_prev, from_next)
    from_down = shifted(jnp.maximum(found["up"], around[1]), above)
    from_up = shifted(jnp.maximum(found["down"], around[2]), below)
    best = jnp.maximum(jnp.maximum(best, found["own"]), around[0])
    best = jnp.maximum(best, jnp.where(row < last_row, from_down, LOW))
    best = jnp.maximum(best, jnp.where(row > 0, from_up, LOW))
    position = lax.broadcasted_iota(jnp.int32, (blocks, count), 1)
    return jnp.where(position < block_rows[:, None], jnp.maximum(1.0 + best, 0.0) - 1.0, 0.0)


def solution(mesh):
    placed = (P(AXES, None, None), P(AXES), P(AXES))
    return jax.shard_map(body, mesh=mesh, in_specs=placed, out_specs=P(AXES, None), check_vma=False)
```

```python
import functools

import jax
import jax.numpy as jnp
from jax import lax
from jax.experimental import pallas as pl
from jax.experimental.pallas import tpu as pltpu
from jax.sharding import PartitionSpec as P

AXES = ("gx", "gy")
ROW = 4
LOW = -4.0
EPSILON = 1e-06
VMEM = 20 * 1024 * 1024
TAIL = 16
DIGIT = 32
BLOCKS, COUNT = 8, 128

OWN, NEXT, PREV, UP, DOWN, UP_NEXT, DOWN_PREV = range(0, 56, 8)
ONE, LEFT_HALF, EVEN, ODD, EVEN_FIRST, ODD_LAST, EVEN_BETWEEN, ODD_BETWEEN = range(56, 64)


def shifted(array, pairs):
    return lax.ppermute(array, AXES, pairs)


def smem():
    return pl.BlockSpec(memory_space=pltpu.SMEM)


def vmem():
    return pl.BlockSpec(memory_space=pltpu.VMEM)


def unit_kernel(cluster, live, embeddings, units):
    blocks, count, width = embeddings.shape
    position = lax.broadcasted_iota(jnp.int32, (count, 1), 0)

    def normalize(b, carry):
        values = embeddings[b].astype(jnp.float32)
        factor = lax.rsqrt(jnp.sum(values * values, axis=-1, keepdims=True) + EPSILON)
        unit = values * factor
        units[pl.ds(pl.multiple_of(b * count, count), count)] = jnp.where(
            position < live[b], unit, unit[0:1]
        ).astype(jnp.bfloat16)
        return carry

    lax.fori_loop(0, blocks, normalize, 0)
    rows = lax.broadcasted_iota(jnp.int32, (TAIL, width), 0)
    columns = lax.broadcasted_iota(jnp.int32, (TAIL, width), 1)
    digits = jnp.zeros((TAIL, width), jnp.float32)
    for j in range(blocks):
        high = lax.div(cluster[j] + 1, DIGIT)
        low = cluster[j] + 1 - high * DIGIT
        digit = jnp.where(rows == 0, high, jnp.where(rows == 1, low, 0)).astype(jnp.float32)
        digits = jnp.where(columns == j, digit, digits)
    units[blocks * count:blocks * count + TAIL] = digits.astype(jnp.bfloat16)


def normalize(embeddings, cluster, live):
    blocks, count, width = embeddings.shape
    return pl.pallas_call(
        unit_kernel,
        out_shape=jax.ShapeDtypeStruct((blocks * count + TAIL, width), jnp.bfloat16),
        in_specs=[smem(), smem(), vmem()],
        out_specs=vmem(),
        compiler_params=pltpu.CompilerParams(vmem_limit_bytes=VMEM),
        cost_estimate=pl.CostEstimate(flops=4 * embeddings.size, bytes_accessed=4 * embeddings.size, transcendentals=0),
    )(cluster, live, embeddings)


def ids_of(units, blocks):
    digits = units[-TAIL:-TAIL + 2, :blocks].astype(jnp.float32)
    return (digits[0] * DIGIT + digits[1]).astype(jnp.int32)


def own_kernel(cluster, live, units, best):
    blocks, count = best.shape
    rows = lax.broadcasted_iota(jnp.int32, (count, count), 0)
    columns = lax.broadcasted_iota(jnp.int32, (count, count), 1)
    other = units[:blocks * count]

    def chunk(i, carry):
        similar = lax.dot_general(
            units[pl.ds(pl.multiple_of(2 * i * count, 2 * count), 2 * count)], other,
            (((1,), (1,)), ((), ())), preferred_element_type=jnp.float32,
        )
        for k in range(2):
            a = 2 * i + k
            top = None
            for j in range(blocks):
                part = similar[k * count:(k + 1) * count, j * count:(j + 1) * count]
                part = part + jnp.where(cluster[a] == cluster[j], 0.0, LOW)
                hidden = (a == j) & ((rows == columns) | (columns >= live[j]))
                part = jnp.where(hidden, LOW, part)
                top = part if top is None else jnp.maximum(top, part)
            best[pl.ds(a, 1)] = jnp.max(top.T, axis=0, keepdims=True)
        return carry

    lax.fori_loop(0, blocks // 2, chunk, 0)


def own_tile(units, cluster, live):
    blocks, count, width = BLOCKS, COUNT, units.shape[1]
    return pl.pallas_call(
        own_kernel,
        out_shape=jax.ShapeDtypeStruct((blocks, count), jnp.float32),
        in_specs=[smem(), smem(), vmem()],
        out_specs=vmem(),
        compiler_params=pltpu.CompilerParams(vmem_limit_bytes=VMEM),
        cost_estimate=pl.CostEstimate(
            flops=2 * (blocks * count) ** 2 * width, bytes_accessed=2 * blocks * count * width, transcendentals=0
        ),
    )(cluster, live, units)


def pairs_kernel(parts, jobs, items, ids, *refs):
    arrays, outs = refs[:len(parts)], refs[len(parts):]
    for out in outs:
        out[...] = jnp.full(out.shape, LOW, jnp.float32)
    for first, second, flag in jobs:
        a, b = arrays[first], arrays[second]
        a_item, a_base, a_offset = parts[first]
        b_item, b_base, b_offset = parts[second]
        a_out, b_out = outs[items.index(a_item)], outs[items.index(b_item)]
        count, b_blocks = COUNT, BLOCKS

        @pl.when(ids[flag] > 0)
        def _(a=a, b=b, a_out=a_out, b_out=b_out, a_base=a_base, b_base=b_base,
              a_offset=a_offset, b_offset=b_offset, b_blocks=b_blocks):
            a0 = a_base + a_offset
            b0 = b_base + b_offset
            least, most = ids[b0], ids[b0 + b_blocks - 1]

            def chunk(i, carry):
                meets = (ids[a0 + 2 * i + 1] >= least) & (ids[a0 + 2 * i] <= most)

                @pl.when(meets)
                def _():
                    similar = lax.dot_general(
                        a[pl.ds(pl.multiple_of(2 * i * count, 2 * count), 2 * count)], b[:b_blocks * count],
                        (((1,), (1,)), ((), ())), preferred_element_type=jnp.float32,
                    )
                    tops = [None, None]
                    for j in range(b_blocks):
                        column = None
                        for k in range(2):
                            part = similar[k * count:(k + 1) * count, j * count:(j + 1) * count]
                            part = part + jnp.where(ids[a0 + 2 * i + k] == ids[b0 + j], 0.0, LOW)
                            tops[k] = part if tops[k] is None else jnp.maximum(tops[k], part)
                            column = part if column is None else jnp.maximum(column, part)
                        here = pl.ds(b_offset + j, 1)
                        b_out[here] = jnp.maximum(b_out[here], jnp.max(column, axis=0, keepdims=True))
                    for k in range(2):
                        here = pl.ds(a_offset + 2 * i + k, 1)
                        a_out[here] = jnp.maximum(a_out[here], jnp.max(tops[k].T, axis=0, keepdims=True))

                return carry

            lax.fori_loop(0, BLOCKS // 2, chunk, 0)


def compare(ids, parts, jobs):
    items = []
    for _, item, _, _ in parts:
        if item not in items:
            items.append(item)
    arrays = [part[0] for part in parts]
    blocks, count = BLOCKS, COUNT
    flops = len(jobs) * 2 * (blocks * count) ** 2 * arrays[0].shape[1]
    found = pl.pallas_call(
        functools.partial(pairs_kernel, [part[1:] for part in parts], jobs, items),
        out_shape=[jax.ShapeDtypeStruct((blocks, count), jnp.float32) for _ in items],
        in_specs=[smem()] + [vmem() for _ in arrays],
        out_specs=[vmem() for _ in items],
        compiler_params=pltpu.CompilerParams(vmem_limit_bytes=VMEM),
        cost_estimate=pl.CostEstimate(
            flops=flops, bytes_accessed=sum(2 * a.size for a in arrays), transcendentals=0
        ),
    )(ids, *arrays)
    return dict(zip(items, found))


def merged(*results):
    total = {}
    for result in results:
        for item, value in result.items():
            total[item] = jnp.maximum(total[item], value) if item in total else value
    return total


def ring(devices, by, rows=None):
    return [
        (row * ROW + x, row * ROW + (x + by) % ROW)
        for row in range(devices // ROW) if rows is None or rows(row) for x in range(ROW)
    ]


def column(devices, by, rows=None):
    return [
        (i, i + by * ROW) for i in range(devices)
        if 0 <= i + by * ROW < devices and (rows is None or rows((i + by * ROW) // ROW))
    ]


def body(embeddings, block_cluster, block_rows):
    minor = lax.axis_size(AXES[1])
    devices = lax.axis_size(AXES[0]) * minor
    blocks, count, _ = embeddings.shape
    major = lax.axis_index(AXES[0])
    me = lax.axis_index(AXES).astype(jnp.int32)
    x, row = me % ROW, me // ROW
    last_row = devices // ROW - 1
    even_site = major % 2 == 0

    def even(r):
        return (r * ROW // minor) % 2 == 0

    def odd(r):
        return not even(r)

    right, left = ring(devices, 1), ring(devices, -1)
    below, above = column(devices, 1), column(devices, -1)

    early, late = even_site & (x == 0), ~even_site & (x == ROW - 1)
    between = (x == 1) | (x == 2)
    flags = jnp.stack([
        x >= 0, x < 2, even_site, ~even_site, early, late, even_site & between, ~even_site & between
    ]).astype(jnp.int32)

    units = normalize(embeddings, block_cluster, block_rows)
    up, down = shifted(units, below), shifted(units, above)
    nxt, prv = shifted(units, left), shifted(units, right)
    best = own_tile(units, block_cluster, block_rows)
    up, down, nxt, prv, best = lax.optimization_barrier((up, down, nxt, prv, best))
    up_next_even = shifted(up, ring(devices, -1, even))
    up_next_odd = shifted(nxt, column(devices, 1, odd))
    down_prev_even = shifted(jnp.where(x == ROW - 1, up, down), ring(devices, 1, even))
    down_prev_odd = shifted(jnp.where(x == ROW - 1, nxt, prv), column(devices, -1, odd))
    near = [ids_of(units, blocks), ids_of(nxt, blocks), ids_of(prv, blocks), ids_of(up, blocks), ids_of(down, blocks)]
    far = [
        jnp.where(even_site, ids_of(up_next_even, blocks), ids_of(up_next_odd, blocks)),
        jnp.where(even_site, ids_of(down_prev_even, blocks), ids_of(down_prev_odd, blocks)),
    ]
    near_ids = jnp.concatenate(near + [jnp.zeros((2 * blocks,), jnp.int32), flags])
    ids = jnp.concatenate(near + far + [flags])

    first = compare(
        near_ids, [(units, "own", OWN, 0), (nxt, "next", NEXT, 0), (prv, "prev", PREV, 0), (up, "up", UP, 0)],
        [(0, 1, ONE), (1, 2, LEFT_HALF), (0, 3, ONE), (1, 3, ONE), (2, 3, ONE)],
    )
    second = compare(
        ids,
        [
            (prv, "prev", PREV, 0), (up, "up", UP, 0), (down, "down", DOWN, 0),
            (up_next_even, "up_next", UP_NEXT, 0), (down_prev_even, "down_prev", DOWN_PREV, 0),
            (up_next_odd, "up_next", UP_NEXT, 0), (down_prev_odd, "down_prev", DOWN_PREV, 0),
        ],
        [
            (0, 3, EVEN), (2, 3, EVEN), (3, 4, EVEN_BETWEEN), (2, 4, EVEN_FIRST),
            (0, 5, ODD), (2, 5, ODD), (5, 6, ODD_BETWEEN), (1, 6, ODD_LAST),
        ],
    )
    found = merged(first, second)
    none = jnp.full((blocks, count), LOW, jnp.float32)
    from_prev = shifted(
        jnp.stack([found["next"], found["up_next"], jnp.where(late, found["down_prev"], none)]), right
    )
    from_next = shifted(
        jnp.stack([
            found["prev"], jnp.where(early, found["down_prev"], none),
            jnp.where(early | late, none, found["down_prev"]),
        ]), left
    )
    around = jnp.maximum(from_prev, from_next)
    from_down = shifted(jnp.maximum(found["up"], around[1]), above)
    from_up = shifted(jnp.maximum(found["down"], around[2]), below)
    best = jnp.maximum(jnp.maximum(best, found["own"]), around[0])
    best = jnp.maximum(best, jnp.where(row < last_row, from_down, LOW))
    best = jnp.maximum(best, jnp.where(row > 0, from_up, LOW))
    position = lax.broadcasted_iota(jnp.int32, (blocks, count), 1)
    return jnp.where(position < block_rows[:, None], jnp.maximum(1.0 + best, 0.0) - 1.0, 0.0)


def solution(mesh):
    placed = (P(AXES, None, None), P(AXES), P(AXES))
    return jax.shard_map(body, mesh=mesh, in_specs=placed, out_specs=P(AXES, None), check_vma=False)
```

```python
import functools

import jax
import jax.numpy as jnp
from jax import lax
from jax.experimental import pallas as pl
from jax.experimental.pallas import tpu as pltpu
from jax.sharding import PartitionSpec as P

AXES = ("gx", "gy")
ROW = 4
LOW = -4.0
EPSILON = 1e-06
VMEM = 60 * 1024 * 1024
TAIL = 16
DIGIT = 32
BLOCKS, COUNT = 8, 128

ONE, LEFT_HALF, EVEN, ODD, EVEN_FIRST, ODD_LAST, EVEN_BETWEEN, ODD_BETWEEN, EVEN_LEFT, ODD_LEFT = range(10)


def shifted(array, pairs):
    return lax.ppermute(array, AXES, pairs)


def smem():
    return pl.BlockSpec(memory_space=pltpu.SMEM)


def anywhere():
    return pl.BlockSpec(memory_space=pl.ANY)


def vmem():
    return pl.BlockSpec(memory_space=pltpu.VMEM)


def unit_kernel(cluster_in, live_in, embeddings, out, given, units, cluster, live, small, arrive, leave):
    blocks, count, width = given.shape
    scalars = [
        pltpu.make_async_copy(cluster_in, cluster, small.at[0]), pltpu.make_async_copy(live_in, live, small.at[1])
    ]
    reads = [pltpu.make_async_copy(embeddings.at[b], given.at[b], arrive.at[b]) for b in range(blocks)]
    spans = [pl.ds(b * count, count) for b in range(blocks)] + [pl.ds(blocks * count, TAIL)]
    writes = [pltpu.make_async_copy(units.at[span], out.at[span], leave.at[b]) for b, span in enumerate(spans)]
    for copy in scalars + reads:
        copy.start()
    for copy in scalars:
        copy.wait()
    rows = lax.broadcasted_iota(jnp.int32, (TAIL, width), 0)
    columns = lax.broadcasted_iota(jnp.int32, (TAIL, width), 1)
    digits = jnp.zeros((TAIL, width), jnp.float32)
    for j in range(blocks):
        high = lax.div(cluster[j] + 1, DIGIT)
        low = cluster[j] + 1 - high * DIGIT
        digit = jnp.where(rows == 0, high, jnp.where(rows == 1, low, 0)).astype(jnp.float32)
        digits = jnp.where(columns == j, digit, digits)
    units[spans[blocks]] = digits.astype(jnp.bfloat16)
    writes[blocks].start()
    position = lax.broadcasted_iota(jnp.int32, (count, 1), 0)
    for b in range(blocks):
        reads[b].wait()
        values = given[b].astype(jnp.float32)
        factor = lax.rsqrt(jnp.sum(values * values, axis=-1, keepdims=True) + EPSILON)
        unit = values * factor
        units[spans[b]] = jnp.where(position < live[b], unit, unit[0:1]).astype(jnp.bfloat16)
        writes[b].start()
    for copy in writes:
        copy.wait()


def normalize(embeddings, cluster, live):
    blocks, count, width = embeddings.shape
    return pl.pallas_call(
        unit_kernel,
        out_shape=jax.ShapeDtypeStruct((blocks * count + TAIL, width), jnp.bfloat16),
        in_specs=[anywhere()] * 3,
        out_specs=anywhere(),
        scratch_shapes=[
            pltpu.VMEM(embeddings.shape, jnp.bfloat16),
            pltpu.VMEM((blocks * count + TAIL, width), jnp.bfloat16),
            pltpu.SMEM((blocks,), jnp.int32),
            pltpu.SMEM((blocks,), jnp.int32),
            pltpu.SemaphoreType.DMA((2,)),
            pltpu.SemaphoreType.DMA((blocks,)),
            pltpu.SemaphoreType.DMA((blocks + 1,)),
        ],
        compiler_params=pltpu.CompilerParams(vmem_limit_bytes=VMEM),
        cost_estimate=pl.CostEstimate(flops=4 * embeddings.size, bytes_accessed=4 * embeddings.size, transcendentals=0),
    )(cluster, live, embeddings)


def own_kernel(cluster, live, units, best):
    blocks, count = best.shape
    rows = lax.broadcasted_iota(jnp.int32, (count, count), 0)
    columns = lax.broadcasted_iota(jnp.int32, (count, count), 1)
    other = units[:blocks * count]

    def chunk(i, carry):
        similar = lax.dot_general(
            units[pl.ds(pl.multiple_of(2 * i * count, 2 * count), 2 * count)], other,
            (((1,), (1,)), ((), ())), preferred_element_type=jnp.float32,
        )
        for k in range(2):
            a = 2 * i + k
            top = None
            for j in range(blocks):
                part = similar[k * count:(k + 1) * count, j * count:(j + 1) * count]
                part = part + jnp.where(cluster[a] == cluster[j], 0.0, LOW)
                hidden = (a == j) & ((rows == columns) | (columns >= live[j]))
                part = jnp.where(hidden, LOW, part)
                top = part if top is None else jnp.maximum(top, part)
            best[pl.ds(a, 1)] = jnp.max(top.T, axis=0, keepdims=True)
        return carry

    lax.fori_loop(0, blocks // 2, chunk, 0)


def own_tile(units, cluster, live):
    blocks, count, width = BLOCKS, COUNT, units.shape[1]
    return pl.pallas_call(
        own_kernel,
        out_shape=jax.ShapeDtypeStruct((blocks, count), jnp.float32),
        in_specs=[smem(), smem(), vmem()],
        out_specs=vmem(),
        compiler_params=pltpu.CompilerParams(vmem_limit_bytes=VMEM),
        cost_estimate=pl.CostEstimate(
            flops=2 * (blocks * count) ** 2 * width, bytes_accessed=2 * blocks * count * width, transcendentals=0
        ),
    )(cluster, live, units)


def pairs_kernel(parts, jobs, items, begun, flags, *refs):
    many = len(parts)
    arrays, refs = refs[:many], refs[many:]
    starts, refs = refs[:len(begun)], refs[len(begun):]
    outs, refs = refs[:len(items)], refs[len(items):]
    held, refs = refs[:many], refs[many:]
    tails, listed, ids, arrived, came, moved, seen, rows_best = refs
    count = COUNT
    ends = [
        pltpu.make_async_copy(arrays[i].at[pl.ds(BLOCKS * count, TAIL), pl.ds(0, 128)], tails.at[i], came.at[i])
        for i in range(many)
    ]
    copies = [
        pltpu.make_async_copy(arrays[i].at[pl.ds(0, BLOCKS * count)], held[i], arrived.at[i]) for i in range(many)
    ]
    for end in ends:
        end.start()
    for item, out in zip(items, outs):
        if item in begun:
            out[...] = starts[begun.index(item)][...]
        else:
            out[...] = jnp.full(out.shape, LOW, jnp.float32)
    for i, end in enumerate(ends):
        end.wait()
        digits = tails[i].astype(jnp.float32)
        listed[i:i + 1] = (digits[0:1] * DIGIT + digits[1:2]).astype(jnp.int32)
    move = pltpu.make_async_copy(listed, ids, moved.at[0])
    move.start()
    move.wait()
    wanted, needed = [], [jnp.bool_(False)] * many
    for first, second, flag in jobs:
        want = (flags[flag] > 0) & (ids[first, BLOCKS - 1] >= ids[second, 0])
        want = want & (ids[first, 0] <= ids[second, BLOCKS - 1])
        wanted.append(want)
        for i in (first, second):
            needed[i] = needed[i] | want
    for i in range(many):
        seen[i] = 0
        pl.when(needed[i])(copies[i].start)
    for (first, second, _), want in zip(jobs, wanted):

        @pl.when(want)
        def _(first=first, second=second):
            for i in (first, second):

                @pl.when(seen[i] == 0)
                def _(i=i):
                    copies[i].wait()
                    seen[i] = 1

            a, b = held[first], held[second]
            a_out, b_out = outs[items.index(parts[first])], outs[items.index(parts[second])]
            tops = rows_best
            tops[...] = jnp.full(tops.shape, LOW, jnp.float32)

            def chunk(i, carry):
                low, high = ids[second, 2 * i], ids[second, 2 * i + 1]
                meets = (high >= ids[first, 0]) & (low <= ids[first, BLOCKS - 1])
                same = (low == high) & (ids[first, 0] == low) & (ids[first, BLOCKS - 1] == low)

                def work(hide):
                    similar = lax.dot_general(
                        a[...], b[pl.ds(pl.multiple_of(2 * i * count, 2 * count), 2 * count)],
                        (((1,), (1,)), ((), ())), preferred_element_type=jnp.float32,
                    )
                    columns = [None, None]
                    for j in range(BLOCKS):
                        here = slice(j * count, (j + 1) * count)
                        top = tops[here]
                        for k in range(2):
                            part = similar[here, k * count:(k + 1) * count]
                            if hide:
                                part = part + jnp.where(ids[first, j] == ids[second, 2 * i + k], 0.0, LOW)
                            top = jnp.maximum(top, part)
                            part = jnp.max(part.reshape(count // 8, 8, count), axis=0)
                            columns[k] = part if columns[k] is None else jnp.maximum(columns[k], part)
                        tops[here] = top
                    for k in range(2):
                        here = pl.ds(2 * i + k, 1)
                        b_out[here] = jnp.maximum(b_out[here], jnp.max(columns[k], axis=0, keepdims=True))

                pl.when(same)(lambda: work(False))
                pl.when(meets & jnp.logical_not(same))(lambda: work(True))
                return carry

            lax.fori_loop(0, BLOCKS // 2, chunk, 0)
            for j in range(BLOCKS):
                top = jnp.max(tops[j * count:(j + 1) * count].T, axis=0, keepdims=True)
                a_out[j:j + 1] = jnp.maximum(a_out[j:j + 1], top)


def compare(flags, parts, jobs, begun):
    items = []
    for _, item in parts:
        if item not in items:
            items.append(item)
    known = [item for item in items if item in begun]
    arrays = [part[0] for part in parts]
    many, width = len(arrays), arrays[0].shape[1]
    found = pl.pallas_call(
        functools.partial(pairs_kernel, [part[1] for part in parts], jobs, items, known),
        out_shape=[jax.ShapeDtypeStruct((BLOCKS, COUNT), jnp.float32) for _ in items],
        in_specs=[smem()] + [anywhere() for _ in arrays] + [vmem() for _ in known],
        out_specs=[vmem() for _ in items],
        scratch_shapes=[pltpu.VMEM((BLOCKS * COUNT, width), jnp.bfloat16) for _ in arrays]
        + [
            pltpu.VMEM((many, TAIL, 128), jnp.bfloat16),
            pltpu.VMEM((8, 128), jnp.int32),
            pltpu.SMEM((8, 128), jnp.int32),
            pltpu.SemaphoreType.DMA((many,)),
            pltpu.SemaphoreType.DMA((many,)),
            pltpu.SemaphoreType.DMA((1,)),
            pltpu.SMEM((many,), jnp.int32),
            pltpu.VMEM((BLOCKS * COUNT, COUNT), jnp.float32),
        ],
        compiler_params=pltpu.CompilerParams(vmem_limit_bytes=VMEM),
        cost_estimate=pl.CostEstimate(
            flops=len(jobs) * 2 * (BLOCKS * COUNT) ** 2 * width,
            bytes_accessed=sum(2 * a.size for a in arrays), transcendentals=0,
        ),
    )(flags, *arrays, *[begun[item] for item in known])
    return {**begun, **dict(zip(items, found))}


def corner_kernel(flags, down, up, out, held, arrive, leave):
    spans = [pl.ds(b * COUNT, COUNT) for b in range(BLOCKS)] + [pl.ds(BLOCKS * COUNT, TAIL)]
    reads = [pltpu.make_async_copy(up.at[span], held.at[span], arrive.at[i]) for i, span in enumerate(spans)]
    writes = [pltpu.make_async_copy(held.at[span], out.at[span], leave.at[i]) for i, span in enumerate(spans)]

    @pl.when(flags[0] > 0)
    def _():
        for read in reads:
            read.start()
        for read, write in zip(reads, writes):
            read.wait()
            write.start()
        for write in writes:
            write.wait()


def with_corner(last, down, up):
    return pl.pallas_call(
        corner_kernel,
        out_shape=jax.ShapeDtypeStruct(down.shape, down.dtype),
        in_specs=[smem(), anywhere(), anywhere()],
        out_specs=anywhere(),
        scratch_shapes=[
            pltpu.VMEM(down.shape, down.dtype),
            pltpu.SemaphoreType.DMA((BLOCKS + 1,)),
            pltpu.SemaphoreType.DMA((BLOCKS + 1,)),
        ],
        input_output_aliases={1: 0},
        compiler_params=pltpu.CompilerParams(vmem_limit_bytes=VMEM),
        cost_estimate=pl.CostEstimate(flops=0, bytes_accessed=4 * down.size, transcendentals=0),
    )(last, down, up)


def ring(devices, by, rows=None):
    return [
        (row * ROW + x, row * ROW + (x + by) % ROW)
        for row in range(devices // ROW) if rows is None or rows(row) for x in range(ROW)
    ]


def column(devices, by, rows=None):
    return [
        (i, i + by * ROW) for i in range(devices)
        if 0 <= i + by * ROW < devices and (rows is None or rows((i + by * ROW) // ROW))
    ]


def body(embeddings, block_cluster, block_rows):
    minor = lax.axis_size(AXES[1])
    devices = lax.axis_size(AXES[0]) * minor
    blocks, count, _ = embeddings.shape
    major = lax.axis_index(AXES[0])
    me = lax.axis_index(AXES).astype(jnp.int32)
    x, row = me % ROW, me // ROW
    last_row = devices // ROW - 1
    even_site = major % 2 == 0

    def even(r):
        return (r * ROW // minor) % 2 == 0

    def odd(r):
        return not even(r)

    right, left = ring(devices, 1), ring(devices, -1)
    below, above = column(devices, 1), column(devices, -1)

    early, late = even_site & (x == 0), ~even_site & (x == ROW - 1)
    between = (x == 1) | (x == 2)
    flags = jnp.stack([
        x >= 0, x < 2, even_site, ~even_site, early, late, even_site & between, ~even_site & between,
        even_site & (x < ROW - 1), ~even_site & (x < ROW - 1),
    ]).astype(jnp.int32)

    units = normalize(embeddings, block_cluster, block_rows)
    up, nxt = shifted(units, below), shifted(units, left)
    down, prv = shifted(units, above), shifted(units, right)
    best = own_tile(units, block_cluster, block_rows)
    up, nxt, best = lax.optimization_barrier((up, nxt, best))
    up_next_even = shifted(up, ring(devices, -1, even))
    up_next_odd = shifted(nxt, column(devices, 1, odd))
    down = with_corner((x == ROW - 1).astype(jnp.int32)[None], down, up)
    down_prev_even = shifted(down, [(i, j) for i, j in ring(devices, 1, even) if j % ROW != ROW - 1])
    down_prev_odd = shifted(prv, [(i, j) for i, j in column(devices, -1, odd) if j % ROW in (1, 2)])
    corner_odd = shifted(nxt, [(i, j) for i, j in column(devices, -1, odd) if j % ROW == ROW - 1])

    found = compare(
        flags, [(nxt, "next"), (units, "own"), (prv, "prev"), (up, "up")],
        [(0, 1, ONE), (0, 3, ONE), (0, 2, LEFT_HALF), (1, 3, ONE), (2, 3, ONE)], {},
    )
    from_prev = shifted(found["next"], right)
    found = compare(
        flags, [(prv, "prev"), (down, "down"), (up_next_even, "up_next"), (up_next_odd, "up_next")],
        [(2, 0, EVEN), (2, 1, EVEN_LEFT), (3, 0, ODD), (3, 1, ODD_LEFT)], found,
    )
    from_next = shifted(found["prev"], left)
    found = compare(
        flags,
        [
            (up, "up"), (down, "down"), (up_next_even, "up_next"), (down_prev_even, "down_prev"),
            (up_next_odd, "up_next"), (down_prev_odd, "down_prev"), (corner_odd, "down_prev"),
        ],
        [(2, 3, EVEN_BETWEEN), (1, 3, EVEN_FIRST), (4, 5, ODD_BETWEEN), (0, 6, ODD_LAST)], found,
    )
    from_below = shifted(found["up"], above)
    from_above = shifted(found["down"], below)
    rows = devices // ROW
    sites = [(r, c) for r in range(rows) for c in range(ROW)]
    from_below_prev = shifted(
        found["up_next"], [(r * ROW + c, (r - 1) * ROW + (c + 1) % ROW) for r, c in sites if r > 0]
    )
    from_corner = shifted(
        found["down_prev"],
        [(r * ROW + c, (r + 1) * ROW + c - 1) for r, c in sites if r + 1 < rows and c in (1, 2)]
        + [(r * ROW, r * ROW - 1) for r in range(1, rows) if even(r)],
    )
    from_last = shifted(
        found["down_prev"], [(r * ROW + ROW - 1, (r + 1) * ROW) for r in range(rows - 1) if odd(r)]
    )
    has_below, has_above = row < last_row, row > 0
    parity_below = ((row + 1) * ROW // minor) % 2
    parity_above = (jnp.maximum(row - 1, 0) * ROW // minor) % 2
    best = jnp.maximum(jnp.maximum(best, found["own"]), jnp.maximum(from_prev, from_next))
    for there, value in (
        (has_below, from_below),
        (has_above, from_above),
        (has_below, from_below_prev),
        ((has_above & (x < 2)) | (has_below & (x == ROW - 1) & (parity_below == 0)), from_corner),
        (has_above & (x == 0) & (parity_above == 1), from_last),
    ):
        best = jnp.maximum(best, jnp.where(there, value, LOW))
    position = lax.broadcasted_iota(jnp.int32, (blocks, count), 1)
    return jnp.where(position < block_rows[:, None], jnp.maximum(1.0 + best, 0.0) - 1.0, 0.0)


def solution(mesh):
    placed = (P(AXES, None, None), P(AXES), P(AXES))
    return jax.shard_map(body, mesh=mesh, in_specs=placed, out_specs=P(AXES, None), check_vma=False)
```

```python
import functools

import jax
import jax.numpy as jnp
from jax import lax
from jax.experimental import pallas as pl
from jax.experimental.pallas import tpu as pltpu
from jax.sharding import PartitionSpec as P

AXES = ("gx", "gy")
ROW = 4
LOW = -4.0
EPSILON = 1e-06
VMEM = 60 * 1024 * 1024
TAIL = 16
DIGIT = 32
BLOCKS, COUNT = 8, 128

ONE, LEFT_HALF, EVEN, ODD, EVEN_FIRST, ODD_LAST, EVEN_BETWEEN, ODD_BETWEEN, EVEN_LEFT, ODD_LEFT = range(10)


def shifted(array, pairs):
    return lax.ppermute(array, AXES, pairs)


def smem():
    return pl.BlockSpec(memory_space=pltpu.SMEM)


def anywhere():
    return pl.BlockSpec(memory_space=pl.ANY)


def vmem():
    return pl.BlockSpec(memory_space=pltpu.VMEM)


def unit_kernel(cluster_in, live_in, embeddings, out, given, units, cluster, live, small, arrive, leave):
    blocks, count, width = given.shape
    scalars = [
        pltpu.make_async_copy(cluster_in, cluster, small.at[0]), pltpu.make_async_copy(live_in, live, small.at[1])
    ]
    reads = [pltpu.make_async_copy(embeddings.at[b], given.at[b], arrive.at[b]) for b in range(blocks)]
    spans = [pl.ds(b * count, count) for b in range(blocks)] + [pl.ds(blocks * count, TAIL)]
    writes = [pltpu.make_async_copy(units.at[span], out.at[span], leave.at[b]) for b, span in enumerate(spans)]
    for copy in scalars + reads:
        copy.start()
    for copy in scalars:
        copy.wait()
    rows = lax.broadcasted_iota(jnp.int32, (TAIL, width), 0)
    columns = lax.broadcasted_iota(jnp.int32, (TAIL, width), 1)
    digits = jnp.zeros((TAIL, width), jnp.float32)
    for j in range(blocks):
        high = lax.div(cluster[j] + 1, DIGIT)
        low = cluster[j] + 1 - high * DIGIT
        digit = jnp.where(rows == 0, high, jnp.where(rows == 1, low, 0)).astype(jnp.float32)
        digits = jnp.where(columns == j, digit, digits)
    units[spans[blocks]] = digits.astype(jnp.bfloat16)
    writes[blocks].start()
    position = lax.broadcasted_iota(jnp.int32, (count, 1), 0)
    for b in range(blocks):
        reads[b].wait()
        values = given[b].astype(jnp.float32)
        factor = lax.rsqrt(jnp.sum(values * values, axis=-1, keepdims=True) + EPSILON)
        unit = values * factor
        units[spans[b]] = jnp.where(position < live[b], unit, unit[0:1]).astype(jnp.bfloat16)
        writes[b].start()
    for copy in writes:
        copy.wait()


def normalize(embeddings, cluster, live):
    blocks, count, width = embeddings.shape
    return pl.pallas_call(
        unit_kernel,
        out_shape=jax.ShapeDtypeStruct((blocks * count + TAIL, width), jnp.bfloat16),
        in_specs=[anywhere()] * 3,
        out_specs=anywhere(),
        scratch_shapes=[
            pltpu.VMEM(embeddings.shape, jnp.bfloat16),
            pltpu.VMEM((blocks * count + TAIL, width), jnp.bfloat16),
            pltpu.SMEM((blocks,), jnp.int32),
            pltpu.SMEM((blocks,), jnp.int32),
            pltpu.SemaphoreType.DMA((2,)),
            pltpu.SemaphoreType.DMA((blocks,)),
            pltpu.SemaphoreType.DMA((blocks + 1,)),
        ],
        compiler_params=pltpu.CompilerParams(vmem_limit_bytes=VMEM),
        cost_estimate=pl.CostEstimate(flops=4 * embeddings.size, bytes_accessed=4 * embeddings.size, transcendentals=0),
    )(cluster, live, embeddings)


def own_kernel(cluster, live, units, best):
    blocks, count = best.shape
    rows = lax.broadcasted_iota(jnp.int32, (count, count), 0)
    columns = lax.broadcasted_iota(jnp.int32, (count, count), 1)
    other = units[:blocks * count]

    def chunk(i, carry):
        similar = lax.dot_general(
            units[pl.ds(pl.multiple_of(2 * i * count, 2 * count), 2 * count)], other,
            (((1,), (1,)), ((), ())), preferred_element_type=jnp.float32,
        )
        for k in range(2):
            a = 2 * i + k
            top = None
            for j in range(blocks):
                part = similar[k * count:(k + 1) * count, j * count:(j + 1) * count]
                part = part + jnp.where(cluster[a] == cluster[j], 0.0, LOW)
                hidden = (a == j) & ((rows == columns) | (columns >= live[j]))
                part = jnp.where(hidden, LOW, part)
                top = part if top is None else jnp.maximum(top, part)
            best[pl.ds(a, 1)] = jnp.max(top.T, axis=0, keepdims=True)
        return carry

    lax.fori_loop(0, blocks // 2, chunk, 0)


def own_tile(units, cluster, live):
    blocks, count, width = BLOCKS, COUNT, units.shape[1]
    return pl.pallas_call(
        own_kernel,
        out_shape=jax.ShapeDtypeStruct((blocks, count), jnp.float32),
        in_specs=[smem(), smem(), vmem()],
        out_specs=vmem(),
        compiler_params=pltpu.CompilerParams(vmem_limit_bytes=VMEM),
        cost_estimate=pl.CostEstimate(
            flops=2 * (blocks * count) ** 2 * width, bytes_accessed=2 * blocks * count * width, transcendentals=0
        ),
    )(cluster, live, units)


def pairs_kernel(parts, count_jobs, items, begun, jobs, flags, *refs):
    many, count = len(parts), COUNT
    arrays, refs = refs[:many], refs[many:]
    starts, refs = refs[:len(begun)], refs[len(begun):]
    outs, refs = refs[:len(items)], refs[len(items):]
    held, best, tails, listed, ids, arrived, came, moved, state, rows_best = refs
    ends = [
        pltpu.make_async_copy(arrays[i].at[pl.ds(BLOCKS * count, TAIL), pl.ds(0, 128)], tails.at[i], came.at[i])
        for i in range(many)
    ]
    for end in ends:
        end.start()
    for k, item in enumerate(items):
        if item in begun:
            best[k] = starts[begun.index(item)][...]
        else:
            best[k] = jnp.full(best.shape[1:], LOW, jnp.float32)
    for i, end in enumerate(ends):
        end.wait()
        digits = tails[i].astype(jnp.float32)
        listed[i:i + 1] = (digits[0:1] * DIGIT + digits[1:2]).astype(jnp.int32)
    move = pltpu.make_async_copy(listed, ids, moved.at[0])
    move.start()
    move.wait()
    for i in range(many):
        state[i] = 0

    def wanted(j):
        first, second = jobs[5 * j], jobs[5 * j + 1]
        meet = (ids[first, BLOCKS - 1] >= ids[second, 0]) & (ids[first, 0] <= ids[second, BLOCKS - 1])
        return meet & (flags[jobs[5 * j + 2]] > 0)

    def mark(j, carry):
        @pl.when(wanted(j))
        def _():
            state[jobs[5 * j]] = 1
            state[jobs[5 * j + 1]] = 1

        return carry

    lax.fori_loop(0, count_jobs, mark, 0)
    for i in range(many):
        copy = pltpu.make_async_copy(arrays[i].at[pl.ds(0, BLOCKS * count)], held.at[i], arrived.at[i])
        pl.when(state[i] > 0)(copy.start)

    def fetched(i):
        @pl.when(state[i] == 1)
        def _():
            pltpu.make_async_copy(arrays[0].at[pl.ds(0, BLOCKS * count)], held.at[i], arrived.at[i]).wait()
            state[i] = 2

    def tile(first, second, a_out, b_out):
        a, b = held.at[first], held.at[second]
        same = (ids[first, 0] == ids[first, BLOCKS - 1]) & (ids[second, 0] == ids[second, BLOCKS - 1])
        same = same & (ids[first, 0] == ids[second, 0])

        @pl.when(same)
        def _():
            columns = [None] * BLOCKS
            for i in range(BLOCKS // 2):
                similar = lax.dot_general(
                    a[2 * i * count:2 * (i + 1) * count], b[...],
                    (((1,), (1,)), ((), ())), preferred_element_type=jnp.float32,
                )
                for k in range(2):
                    top = None
                    for j in range(BLOCKS):
                        part = similar[k * count:(k + 1) * count, j * count:(j + 1) * count]
                        top = part if top is None else jnp.maximum(top, part)
                        part = jnp.max(part.reshape(count // 8, 8, count), axis=0)
                        columns[j] = part if columns[j] is None else jnp.maximum(columns[j], part)
                    here = slice(2 * i + k, 2 * i + k + 1)
                    top = jnp.max(top.T, axis=0, keepdims=True)
                    best[a_out, here] = jnp.maximum(best[a_out, here], top)
            for j in range(BLOCKS):
                here = slice(j, j + 1)
                top = jnp.max(columns[j], axis=0, keepdims=True)
                best[b_out, here] = jnp.maximum(best[b_out, here], top)

        @pl.when(jnp.logical_not(same))
        def _():
            rows_best[...] = jnp.full(rows_best.shape, LOW, jnp.float32)

            def chunk(n, carry):
                i, j = lax.div(n, BLOCKS // 2), lax.rem(n, BLOCKS // 2)
                meet = ids[first, 2 * i + 1] >= ids[second, 2 * j]

                @pl.when(meet & (ids[first, 2 * i] <= ids[second, 2 * j + 1]))
                def _():
                    similar = lax.dot_general(
                        a[pl.ds(pl.multiple_of(2 * i * count, 2 * count), 2 * count)],
                        b[pl.ds(pl.multiple_of(2 * j * count, 2 * count), 2 * count)],
                        (((1,), (1,)), ((), ())), preferred_element_type=jnp.float32,
                    )
                    columns = [None, None]
                    for k in range(2):
                        here = pl.ds(pl.multiple_of((2 * i + k) * count, count), count)
                        top = rows_best[here]
                        for m in range(2):
                            part = similar[k * count:(k + 1) * count, m * count:(m + 1) * count]
                            part = part + jnp.where(ids[first, 2 * i + k] == ids[second, 2 * j + m], 0.0, LOW)
                            top = jnp.maximum(top, part)
                            columns[m] = part if columns[m] is None else jnp.maximum(columns[m], part)
                        rows_best[here] = top
                    for m in range(2):
                        here = pl.ds(2 * j + m, 1)
                        top = jnp.max(columns[m], axis=0, keepdims=True)
                        best[b_out, here] = jnp.maximum(best[b_out, here], top)

                return carry

            lax.fori_loop(0, (BLOCKS // 2) ** 2, chunk, 0)
            for j in range(BLOCKS):
                top = jnp.max(rows_best[j * count:(j + 1) * count].T, axis=0, keepdims=True)
                best[a_out, j:j + 1] = jnp.maximum(best[a_out, j:j + 1], top)

    def job(j, carry):
        @pl.when(wanted(j))
        def _():
            first, second = jobs[5 * j], jobs[5 * j + 1]
            fetched(first)
            fetched(second)
            tile(first, second, jobs[5 * j + 3], jobs[5 * j + 4])

        return carry

    lax.fori_loop(0, count_jobs, job, 0)
    for k, out in enumerate(outs):
        out[...] = best[k]


def compare(flags, parts, jobs, begun):
    items = []
    for _, item in parts:
        if item not in items:
            items.append(item)
    known = [item for item in items if item in begun]
    arrays = [part[0] for part in parts]
    many, width = len(arrays), arrays[0].shape[1]
    listed = jnp.array(
        [v for f, s, flag in jobs for v in (f, s, flag, items.index(parts[f][1]), items.index(parts[s][1]))], jnp.int32
    )
    found = pl.pallas_call(
        functools.partial(pairs_kernel, [part[1] for part in parts], len(jobs), items, known),
        out_shape=[jax.ShapeDtypeStruct((BLOCKS, COUNT), jnp.float32) for _ in items],
        in_specs=[smem(), smem()] + [anywhere() for _ in arrays] + [vmem() for _ in known],
        out_specs=[vmem() for _ in items],
        scratch_shapes=[
            pltpu.VMEM((many, BLOCKS * COUNT, width), jnp.bfloat16),
            pltpu.VMEM((len(items), BLOCKS, COUNT), jnp.float32),
            pltpu.VMEM((many, TAIL, 128), jnp.bfloat16),
            pltpu.VMEM((8, 128), jnp.int32),
            pltpu.SMEM((8, 128), jnp.int32),
            pltpu.SemaphoreType.DMA((many,)),
            pltpu.SemaphoreType.DMA((many,)),
            pltpu.SemaphoreType.DMA((1,)),
            pltpu.SMEM((many,), jnp.int32),
            pltpu.VMEM((BLOCKS * COUNT, COUNT), jnp.float32),
        ],
        compiler_params=pltpu.CompilerParams(vmem_limit_bytes=VMEM),
        cost_estimate=pl.CostEstimate(
            flops=len(jobs) * 2 * (BLOCKS * COUNT) ** 2 * width,
            bytes_accessed=sum(2 * a.size for a in arrays), transcendentals=0,
        ),
    )(listed, flags, *arrays, *[begun[item] for item in known])
    return {**begun, **dict(zip(items, found))}


def corner_kernel(flags, down, up, out, held, arrive, leave):
    spans = [pl.ds(b * COUNT, COUNT) for b in range(BLOCKS)] + [pl.ds(BLOCKS * COUNT, TAIL)]
    reads = [pltpu.make_async_copy(up.at[span], held.at[span], arrive.at[i]) for i, span in enumerate(spans)]
    writes = [pltpu.make_async_copy(held.at[span], out.at[span], leave.at[i]) for i, span in enumerate(spans)]

    @pl.when(flags[0] > 0)
    def _():
        for read in reads:
            read.start()
        for read, write in zip(reads, writes):
            read.wait()
            write.start()
        for write in writes:
            write.wait()


def with_corner(last, down, up):
    return pl.pallas_call(
        corner_kernel,
        out_shape=jax.ShapeDtypeStruct(down.shape, down.dtype),
        in_specs=[smem(), anywhere(), anywhere()],
        out_specs=anywhere(),
        scratch_shapes=[
            pltpu.VMEM(down.shape, down.dtype),
            pltpu.SemaphoreType.DMA((BLOCKS + 1,)),
            pltpu.SemaphoreType.DMA((BLOCKS + 1,)),
        ],
        input_output_aliases={1: 0},
        compiler_params=pltpu.CompilerParams(vmem_limit_bytes=VMEM),
        cost_estimate=pl.CostEstimate(flops=0, bytes_accessed=4 * down.size, transcendentals=0),
    )(last, down, up)


def ring(devices, by, rows=None):
    return [
        (row * ROW + x, row * ROW + (x + by) % ROW)
        for row in range(devices // ROW) if rows is None or rows(row) for x in range(ROW)
    ]


def column(devices, by, rows=None):
    return [
        (i, i + by * ROW) for i in range(devices)
        if 0 <= i + by * ROW < devices and (rows is None or rows((i + by * ROW) // ROW))
    ]


def body(embeddings, block_cluster, block_rows):
    minor = lax.axis_size(AXES[1])
    devices = lax.axis_size(AXES[0]) * minor
    blocks, count, _ = embeddings.shape
    major = lax.axis_index(AXES[0])
    me = lax.axis_index(AXES).astype(jnp.int32)
    x, row = me % ROW, me // ROW
    last_row = devices // ROW - 1
    even_site = major % 2 == 0

    def even(r):
        return (r * ROW // minor) % 2 == 0

    def odd(r):
        return not even(r)

    right, left = ring(devices, 1), ring(devices, -1)
    below, above = column(devices, 1), column(devices, -1)

    early, late = even_site & (x == 0), ~even_site & (x == ROW - 1)
    between = (x == 1) | (x == 2)
    flags = jnp.stack([
        x >= 0, x < 2, even_site, ~even_site, early, late, even_site & between, ~even_site & between,
        even_site & (x < ROW - 1), ~even_site & (x < ROW - 1),
    ]).astype(jnp.int32)

    units = normalize(embeddings, block_cluster, block_rows)
    up, nxt = shifted(units, below), shifted(units, left)
    down, prv = shifted(units, above), shifted(units, right)
    best = own_tile(units, block_cluster, block_rows)
    up, nxt, best = lax.optimization_barrier((up, nxt, best))
    up_next_even = shifted(up, ring(devices, -1, even))
    up_next_odd = shifted(nxt, column(devices, 1, odd))
    down = with_corner((x == ROW - 1).astype(jnp.int32)[None], down, up)
    down_prev_even = shifted(down, [(i, j) for i, j in ring(devices, 1, even) if j % ROW != ROW - 1])
    down_prev_odd = shifted(prv, [(i, j) for i, j in column(devices, -1, odd) if j % ROW in (1, 2)])
    corner_odd = shifted(nxt, [(i, j) for i, j in column(devices, -1, odd) if j % ROW == ROW - 1])

    found = compare(
        flags, [(nxt, "next"), (units, "own"), (prv, "prev"), (up, "up")],
        [(0, 1, ONE), (0, 3, ONE), (0, 2, LEFT_HALF), (1, 3, ONE), (2, 3, ONE)], {},
    )
    found = compare(
        flags, [(prv, "prev"), (down, "down"), (up_next_even, "up_next"), (up_next_odd, "up_next")],
        [(2, 0, EVEN), (2, 1, EVEN_LEFT), (3, 0, ODD), (3, 1, ODD_LEFT)], found,
    )
    found = compare(
        flags,
        [
            (up, "corner"), (down, "down"), (up_next_even, "up_next"), (down_prev_even, "down_prev"),
            (up_next_odd, "up_next"), (down_prev_odd, "down_prev"), (corner_odd, "down_prev"),
        ],
        [(2, 3, EVEN_BETWEEN), (1, 3, EVEN_FIRST), (4, 5, ODD_BETWEEN), (0, 6, ODD_LAST)], found,
    )
    none = jnp.full((blocks, count), LOW, jnp.float32)
    from_prev = shifted(
        jnp.stack([found["next"], found["up_next"], jnp.where(late, found["down_prev"], none)]), right
    )
    from_next = shifted(
        jnp.stack([
            found["prev"], jnp.where(early, found["down_prev"], none),
            jnp.where(early | late, none, found["down_prev"]),
        ]), left
    )
    around = jnp.maximum(from_prev, from_next)
    from_below = shifted(jnp.maximum(jnp.maximum(found["up"], found["corner"]), around[1]), above)
    from_above = shifted(jnp.maximum(found["down"], around[2]), below)
    best = jnp.maximum(jnp.maximum(best, found["own"]), around[0])
    best = jnp.maximum(best, jnp.where(row < last_row, from_below, LOW))
    best = jnp.maximum(best, jnp.where(row > 0, from_above, LOW))
    position = lax.broadcasted_iota(jnp.int32, (blocks, count), 1)
    return jnp.where(position < block_rows[:, None], jnp.maximum(1.0 + best, 0.0) - 1.0, 0.0)


def solution(mesh):
    placed = (P(AXES, None, None), P(AXES), P(AXES))
    return jax.shard_map(body, mesh=mesh, in_specs=placed, out_specs=P(AXES, None), check_vma=False)
```

```python
import functools

import jax
import jax.numpy as jnp
from jax import lax
from jax.experimental import pallas as pl
from jax.experimental.pallas import tpu as pltpu
from jax.sharding import PartitionSpec as P

AXES = ("gx", "gy")
ROW = 4
LOW = -4.0
EPSILON = 1e-06
VMEM = 60 * 1024 * 1024
TAIL = 16
DIGIT = 32
BLOCKS, COUNT = 8, 128

ONE, LEFT_HALF, EVEN, ODD, EVEN_FIRST, ODD_LAST, EVEN_BETWEEN, ODD_BETWEEN, EVEN_LEFT, ODD_LEFT = range(10)


def shifted(array, pairs):
    return lax.ppermute(array, AXES, pairs)


def smem():
    return pl.BlockSpec(memory_space=pltpu.SMEM)


def anywhere():
    return pl.BlockSpec(memory_space=pl.ANY)


def vmem():
    return pl.BlockSpec(memory_space=pltpu.VMEM)


def unit_kernel(cluster_in, live_in, embeddings, out, given, units, cluster, live, small, arrive, leave):
    blocks, count, width = given.shape
    scalars = [
        pltpu.make_async_copy(cluster_in, cluster, small.at[0]), pltpu.make_async_copy(live_in, live, small.at[1])
    ]
    reads = [pltpu.make_async_copy(embeddings.at[b], given.at[b], arrive.at[b]) for b in range(blocks)]
    spans = [pl.ds(b * count, count) for b in range(blocks)] + [pl.ds(blocks * count, TAIL)]
    writes = [pltpu.make_async_copy(units.at[span], out.at[span], leave.at[b]) for b, span in enumerate(spans)]
    for copy in scalars + reads:
        copy.start()
    for copy in scalars:
        copy.wait()
    rows = lax.broadcasted_iota(jnp.int32, (TAIL, width), 0)
    columns = lax.broadcasted_iota(jnp.int32, (TAIL, width), 1)
    digits = jnp.zeros((TAIL, width), jnp.float32)
    for j in range(blocks):
        high = lax.div(cluster[j] + 1, DIGIT)
        low = cluster[j] + 1 - high * DIGIT
        digit = jnp.where(rows == 0, high, jnp.where(rows == 1, low, 0)).astype(jnp.float32)
        digits = jnp.where(columns == j, digit, digits)
    units[spans[blocks]] = digits.astype(jnp.bfloat16)
    writes[blocks].start()
    position = lax.broadcasted_iota(jnp.int32, (count, 1), 0)
    for b in range(blocks):
        reads[b].wait()
        values = given[b].astype(jnp.float32)
        factor = lax.rsqrt(jnp.sum(values * values, axis=-1, keepdims=True) + EPSILON)
        unit = values * factor
        units[spans[b]] = jnp.where(position < live[b], unit, unit[0:1]).astype(jnp.bfloat16)
        writes[b].start()
    for copy in writes:
        copy.wait()


def normalize(embeddings, cluster, live):
    blocks, count, width = embeddings.shape
    return pl.pallas_call(
        unit_kernel,
        out_shape=jax.ShapeDtypeStruct((blocks * count + TAIL, width), jnp.bfloat16),
        in_specs=[anywhere()] * 3,
        out_specs=anywhere(),
        scratch_shapes=[
            pltpu.VMEM(embeddings.shape, jnp.bfloat16),
            pltpu.VMEM((blocks * count + TAIL, width), jnp.bfloat16),
            pltpu.SMEM((blocks,), jnp.int32),
            pltpu.SMEM((blocks,), jnp.int32),
            pltpu.SemaphoreType.DMA((2,)),
            pltpu.SemaphoreType.DMA((blocks,)),
            pltpu.SemaphoreType.DMA((blocks + 1,)),
        ],
        compiler_params=pltpu.CompilerParams(vmem_limit_bytes=VMEM),
        cost_estimate=pl.CostEstimate(flops=4 * embeddings.size, bytes_accessed=4 * embeddings.size, transcendentals=0),
    )(cluster, live, embeddings)


def own_kernel(cluster, live, units, best):
    blocks, count = best.shape
    rows = lax.broadcasted_iota(jnp.int32, (count, count), 0)
    columns = lax.broadcasted_iota(jnp.int32, (count, count), 1)
    other = units[:blocks * count]

    def chunk(i, carry):
        similar = lax.dot_general(
            units[pl.ds(pl.multiple_of(2 * i * count, 2 * count), 2 * count)], other,
            (((1,), (1,)), ((), ())), preferred_element_type=jnp.float32,
        )
        for k in range(2):
            a = 2 * i + k
            top = None
            for j in range(blocks):
                part = similar[k * count:(k + 1) * count, j * count:(j + 1) * count]
                part = part + jnp.where(cluster[a] == cluster[j], 0.0, LOW)
                hidden = (a == j) & ((rows == columns) | (columns >= live[j]))
                part = jnp.where(hidden, LOW, part)
                top = part if top is None else jnp.maximum(top, part)
            best[pl.ds(a, 1)] = jnp.max(top.T, axis=0, keepdims=True)
        return carry

    lax.fori_loop(0, blocks // 2, chunk, 0)


def own_tile(units, cluster, live):
    blocks, count, width = BLOCKS, COUNT, units.shape[1]
    return pl.pallas_call(
        own_kernel,
        out_shape=jax.ShapeDtypeStruct((blocks, count), jnp.float32),
        in_specs=[smem(), smem(), vmem()],
        out_specs=vmem(),
        compiler_params=pltpu.CompilerParams(vmem_limit_bytes=VMEM),
        cost_estimate=pl.CostEstimate(
            flops=2 * (blocks * count) ** 2 * width, bytes_accessed=2 * blocks * count * width, transcendentals=0
        ),
    )(cluster, live, units)


def pairs_kernel(parts, count_jobs, items, begun, jobs, flags, *refs):
    many, count = len(parts), COUNT
    arrays, refs = refs[:many], refs[many:]
    starts, refs = refs[:len(begun)], refs[len(begun):]
    outs, refs = refs[:len(items)], refs[len(items):]
    held, best, tails, listed, ids, arrived, came, moved, state, rows_best = refs
    ends = [
        pltpu.make_async_copy(arrays[i].at[pl.ds(BLOCKS * count, TAIL), pl.ds(0, 128)], tails.at[i], came.at[i])
        for i in range(many)
    ]
    for end in ends:
        end.start()
    for k, item in enumerate(items):
        if item in begun:
            best[k] = starts[begun.index(item)][...]
        else:
            best[k] = jnp.full(best.shape[1:], LOW, jnp.float32)
    for i, end in enumerate(ends):
        end.wait()
        digits = tails[i].astype(jnp.float32)
        listed[i:i + 1] = (digits[0:1] * DIGIT + digits[1:2]).astype(jnp.int32)
    move = pltpu.make_async_copy(listed, ids, moved.at[0])
    move.start()
    move.wait()
    for i in range(many):
        state[i] = 0

    def wanted(j):
        first, second = jobs[5 * j], jobs[5 * j + 1]
        meet = (ids[first, BLOCKS - 1] >= ids[second, 0]) & (ids[first, 0] <= ids[second, BLOCKS - 1])
        return meet & (flags[jobs[5 * j + 2]] > 0)

    def mark(j, carry):
        @pl.when(wanted(j))
        def _():
            state[jobs[5 * j]] = 1
            state[jobs[5 * j + 1]] = 1

        return carry

    lax.fori_loop(0, count_jobs, mark, 0)
    for i in range(many):
        copy = pltpu.make_async_copy(arrays[i].at[pl.ds(0, BLOCKS * count)], held.at[i], arrived.at[i])
        pl.when(state[i] > 0)(copy.start)

    def fetched(i):
        @pl.when(state[i] == 1)
        def _():
            pltpu.make_async_copy(arrays[0].at[pl.ds(0, BLOCKS * count)], held.at[i], arrived.at[i]).wait()
            state[i] = 2

    def tile(first, second, a_out, b_out):
        a, b = held.at[first], held.at[second]
        same = (ids[first, 0] == ids[first, BLOCKS - 1]) & (ids[second, 0] == ids[second, BLOCKS - 1])
        same = same & (ids[first, 0] == ids[second, 0])

        @pl.when(same)
        def _():
            columns = [None] * BLOCKS
            for i in range(BLOCKS // 2):
                similar = lax.dot_general(
                    a[2 * i * count:2 * (i + 1) * count], b[...],
                    (((1,), (1,)), ((), ())), preferred_element_type=jnp.float32,
                )
                for k in range(2):
                    top = None
                    for j in range(BLOCKS):
                        part = similar[k * count:(k + 1) * count, j * count:(j + 1) * count]
                        top = part if top is None else jnp.maximum(top, part)
                        part = jnp.max(part.reshape(count // 8, 8, count), axis=0)
                        columns[j] = part if columns[j] is None else jnp.maximum(columns[j], part)
                    here = slice(2 * i + k, 2 * i + k + 1)
                    top = jnp.max(top.T, axis=0, keepdims=True)
                    best[a_out, here] = jnp.maximum(best[a_out, here], top)
            for j in range(BLOCKS):
                here = slice(j, j + 1)
                top = jnp.max(columns[j], axis=0, keepdims=True)
                best[b_out, here] = jnp.maximum(best[b_out, here], top)

        @pl.when(jnp.logical_not(same))
        def _():
            rows_best[...] = jnp.full(rows_best.shape, LOW, jnp.float32)

            def chunk(n, carry):
                i, j = lax.div(n, BLOCKS // 2), lax.rem(n, BLOCKS // 2)
                meet = ids[first, 2 * i + 1] >= ids[second, 2 * j]

                @pl.when(meet & (ids[first, 2 * i] <= ids[second, 2 * j + 1]))
                def _():
                    similar = lax.dot_general(
                        a[pl.ds(pl.multiple_of(2 * i * count, 2 * count), 2 * count)],
                        b[pl.ds(pl.multiple_of(2 * j * count, 2 * count), 2 * count)],
                        (((1,), (1,)), ((), ())), preferred_element_type=jnp.float32,
                    )
                    columns = [None, None]
                    for k in range(2):
                        here = pl.ds(pl.multiple_of((2 * i + k) * count, count), count)
                        top = rows_best[here]
                        for m in range(2):
                            part = similar[k * count:(k + 1) * count, m * count:(m + 1) * count]
                            part = part + jnp.where(ids[first, 2 * i + k] == ids[second, 2 * j + m], 0.0, LOW)
                            top = jnp.maximum(top, part)
                            columns[m] = part if columns[m] is None else jnp.maximum(columns[m], part)
                        rows_best[here] = top
                    for m in range(2):
                        here = pl.ds(2 * j + m, 1)
                        top = jnp.max(columns[m], axis=0, keepdims=True)
                        best[b_out, here] = jnp.maximum(best[b_out, here], top)

                return carry

            lax.fori_loop(0, (BLOCKS // 2) ** 2, chunk, 0)
            for j in range(BLOCKS):
                top = jnp.max(rows_best[j * count:(j + 1) * count].T, axis=0, keepdims=True)
                best[a_out, j:j + 1] = jnp.maximum(best[a_out, j:j + 1], top)

    def job(j, carry):
        @pl.when(wanted(j))
        def _():
            first, second = jobs[5 * j], jobs[5 * j + 1]
            fetched(first)
            fetched(second)
            tile(first, second, jobs[5 * j + 3], jobs[5 * j + 4])

        return carry

    lax.fori_loop(0, count_jobs, job, 0)
    for k, out in enumerate(outs):
        out[...] = best[k]


def compare(flags, parts, jobs, begun):
    items = []
    for _, item in parts:
        if item not in items:
            items.append(item)
    known = [item for item in items if item in begun]
    arrays = [part[0] for part in parts]
    many, width = len(arrays), arrays[0].shape[1]
    listed = jnp.array(
        [v for f, s, flag in jobs for v in (f, s, flag, items.index(parts[f][1]), items.index(parts[s][1]))], jnp.int32
    )
    found = pl.pallas_call(
        functools.partial(pairs_kernel, [part[1] for part in parts], len(jobs), items, known),
        out_shape=[jax.ShapeDtypeStruct((BLOCKS, COUNT), jnp.float32) for _ in items],
        in_specs=[smem(), smem()] + [anywhere() for _ in arrays] + [vmem() for _ in known],
        out_specs=[vmem() for _ in items],
        scratch_shapes=[
            pltpu.VMEM((many, BLOCKS * COUNT, width), jnp.bfloat16),
            pltpu.VMEM((len(items), BLOCKS, COUNT), jnp.float32),
            pltpu.VMEM((many, TAIL, 128), jnp.bfloat16),
            pltpu.VMEM((8, 128), jnp.int32),
            pltpu.SMEM((8, 128), jnp.int32),
            pltpu.SemaphoreType.DMA((many,)),
            pltpu.SemaphoreType.DMA((many,)),
            pltpu.SemaphoreType.DMA((1,)),
            pltpu.SMEM((many,), jnp.int32),
            pltpu.VMEM((BLOCKS * COUNT, COUNT), jnp.float32),
        ],
        compiler_params=pltpu.CompilerParams(vmem_limit_bytes=VMEM),
        cost_estimate=pl.CostEstimate(
            flops=len(jobs) * 2 * (BLOCKS * COUNT) ** 2 * width,
            bytes_accessed=sum(2 * a.size for a in arrays), transcendentals=0,
        ),
    )(listed, flags, *arrays, *[begun[item] for item in known])
    return {**begun, **dict(zip(items, found))}


def corner_kernel(flags, down, up, out, held, arrive, leave):
    spans = [pl.ds(b * COUNT, COUNT) for b in range(BLOCKS)] + [pl.ds(BLOCKS * COUNT, TAIL)]
    reads = [pltpu.make_async_copy(up.at[span], held.at[span], arrive.at[i]) for i, span in enumerate(spans)]
    writes = [pltpu.make_async_copy(held.at[span], out.at[span], leave.at[i]) for i, span in enumerate(spans)]

    @pl.when(flags[0] > 0)
    def _():
        for read in reads:
            read.start()
        for read, write in zip(reads, writes):
            read.wait()
            write.start()
        for write in writes:
            write.wait()


def with_corner(last, down, up):
    return pl.pallas_call(
        corner_kernel,
        out_shape=jax.ShapeDtypeStruct(down.shape, down.dtype),
        in_specs=[smem(), anywhere(), anywhere()],
        out_specs=anywhere(),
        scratch_shapes=[
            pltpu.VMEM(down.shape, down.dtype),
            pltpu.SemaphoreType.DMA((BLOCKS + 1,)),
            pltpu.SemaphoreType.DMA((BLOCKS + 1,)),
        ],
        input_output_aliases={1: 0},
        compiler_params=pltpu.CompilerParams(vmem_limit_bytes=VMEM),
        cost_estimate=pl.CostEstimate(flops=0, bytes_accessed=4 * down.size, transcendentals=0),
    )(last, down, up)


def ring(devices, by, rows=None):
    return [
        (row * ROW + x, row * ROW + (x + by) % ROW)
        for row in range(devices // ROW) if rows is None or rows(row) for x in range(ROW)
    ]


def column(devices, by, rows=None):
    return [
        (i, i + by * ROW) for i in range(devices)
        if 0 <= i + by * ROW < devices and (rows is None or rows((i + by * ROW) // ROW))
    ]


def body(embeddings, block_cluster, block_rows):
    minor = lax.axis_size(AXES[1])
    devices = lax.axis_size(AXES[0]) * minor
    blocks, count, _ = embeddings.shape
    major = lax.axis_index(AXES[0])
    me = lax.axis_index(AXES).astype(jnp.int32)
    x, row = me % ROW, me // ROW
    last_row = devices // ROW - 1
    even_site = major % 2 == 0

    def even(r):
        return (r * ROW // minor) % 2 == 0

    def odd(r):
        return not even(r)

    right, left = ring(devices, 1), ring(devices, -1)
    below, above = column(devices, 1), column(devices, -1)

    early, late = even_site & (x == 0), ~even_site & (x == ROW - 1)
    between = (x == 1) | (x == 2)
    flags = jnp.stack([
        x >= 0, x < 2, even_site, ~even_site, early, late, even_site & between, ~even_site & between,
        even_site & (x < ROW - 1), ~even_site & (x < ROW - 1),
    ]).astype(jnp.int32)

    units = normalize(embeddings, block_cluster, block_rows)
    up, nxt = shifted(units, below), shifted(units, left)
    down, prv = shifted(units, above), shifted(units, right)
    best = own_tile(units, block_cluster, block_rows)
    up, first_best = lax.optimization_barrier((up, best))
    nxt, second_best = lax.optimization_barrier((nxt, best))
    best = jnp.maximum(first_best, second_best)
    up_next_even = shifted(up, ring(devices, -1, even))
    up_next_odd = shifted(nxt, column(devices, 1, odd))
    down = with_corner((x == ROW - 1).astype(jnp.int32)[None], down, up)
    down_prev_even = shifted(down, [(i, j) for i, j in ring(devices, 1, even) if j % ROW != ROW - 1])
    down_prev_odd = shifted(prv, [(i, j) for i, j in column(devices, -1, odd) if j % ROW in (1, 2)])
    corner_odd = shifted(nxt, [(i, j) for i, j in column(devices, -1, odd) if j % ROW == ROW - 1])

    found = compare(
        flags, [(nxt, "next"), (units, "own"), (prv, "prev"), (up, "up")],
        [(0, 1, ONE), (0, 3, ONE), (0, 2, LEFT_HALF), (1, 3, ONE), (2, 3, ONE)], {},
    )
    found = compare(
        flags, [(prv, "prev"), (down, "down"), (up_next_even, "up_next"), (up_next_odd, "up_next")],
        [(2, 0, EVEN), (2, 1, EVEN_LEFT), (3, 0, ODD), (3, 1, ODD_LEFT)], found,
    )
    found = compare(
        flags,
        [
            (up, "corner"), (down, "down"), (up_next_even, "up_next"), (down_prev_even, "down_prev"),
            (up_next_odd, "up_next"), (down_prev_odd, "down_prev"), (corner_odd, "down_prev"),
        ],
        [(2, 3, EVEN_BETWEEN), (1, 3, EVEN_FIRST), (4, 5, ODD_BETWEEN), (0, 6, ODD_LAST)], found,
    )
    none = jnp.full((blocks, count), LOW, jnp.float32)
    from_prev = shifted(
        jnp.stack([found["next"], found["up_next"], jnp.where(late, found["down_prev"], none)]), right
    )
    from_next = shifted(
        jnp.stack([
            found["prev"], jnp.where(early, found["down_prev"], none),
            jnp.where(early | late, none, found["down_prev"]),
        ]), left
    )
    around = jnp.maximum(from_prev, from_next)
    from_below = shifted(jnp.maximum(jnp.maximum(found["up"], found["corner"]), around[1]), above)
    from_above = shifted(jnp.maximum(found["down"], around[2]), below)
    best = jnp.maximum(jnp.maximum(best, found["own"]), around[0])
    best = jnp.maximum(best, jnp.where(row < last_row, from_below, LOW))
    best = jnp.maximum(best, jnp.where(row > 0, from_above, LOW))
    position = lax.broadcasted_iota(jnp.int32, (blocks, count), 1)
    return jnp.where(position < block_rows[:, None], jnp.maximum(1.0 + best, 0.0) - 1.0, 0.0)


def solution(mesh):
    placed = (P(AXES, None, None), P(AXES), P(AXES))
    return jax.shard_map(body, mesh=mesh, in_specs=placed, out_specs=P(AXES, None), check_vma=False)
```

```python
import functools

import jax
import jax.numpy as jnp
from jax import lax
from jax.experimental import pallas as pl
from jax.experimental.pallas import tpu as pltpu
from jax.sharding import PartitionSpec as P

AXES = ("gx", "gy")
ROW = 4
LOW = -4.0
EPSILON = 1e-06
VMEM = 60 * 1024 * 1024
TAIL = 16
DIGIT = 32
BLOCKS, COUNT = 8, 128

ONE, LEFT_HALF, EVEN, ODD, EVEN_FIRST, ODD_LAST, EVEN_BETWEEN, ODD_BETWEEN, EVEN_LEFT, ODD_LEFT = range(10)


def shifted(array, pairs):
    return lax.ppermute(array, AXES, pairs)


def smem():
    return pl.BlockSpec(memory_space=pltpu.SMEM)


def anywhere():
    return pl.BlockSpec(memory_space=pl.ANY)


def vmem():
    return pl.BlockSpec(memory_space=pltpu.VMEM)


def unit_kernel(cluster_in, live_in, embeddings, out, given, units, cluster, live, small, arrive, leave):
    blocks, count, width = given.shape
    scalars = [
        pltpu.make_async_copy(cluster_in, cluster, small.at[0]), pltpu.make_async_copy(live_in, live, small.at[1])
    ]
    reads = [pltpu.make_async_copy(embeddings.at[b], given.at[b], arrive.at[b]) for b in range(blocks)]
    spans = [pl.ds(b * count, count) for b in range(blocks)] + [pl.ds(blocks * count, TAIL)]
    writes = [pltpu.make_async_copy(units.at[span], out.at[span], leave.at[b]) for b, span in enumerate(spans)]
    for copy in scalars + reads:
        copy.start()
    for copy in scalars:
        copy.wait()
    rows = lax.broadcasted_iota(jnp.int32, (TAIL, width), 0)
    columns = lax.broadcasted_iota(jnp.int32, (TAIL, width), 1)
    digits = jnp.zeros((TAIL, width), jnp.float32)
    for j in range(blocks):
        high = lax.div(cluster[j] + 1, DIGIT)
        low = cluster[j] + 1 - high * DIGIT
        digit = jnp.where(rows == 0, high, jnp.where(rows == 1, low, 0)).astype(jnp.float32)
        digits = jnp.where(columns == j, digit, digits)
    units[spans[blocks]] = digits.astype(jnp.bfloat16)
    writes[blocks].start()
    position = lax.broadcasted_iota(jnp.int32, (count, 1), 0)
    for b in range(blocks):
        reads[b].wait()
        values = given[b].astype(jnp.float32)
        factor = lax.rsqrt(jnp.sum(values * values, axis=-1, keepdims=True) + EPSILON)
        unit = values * factor
        units[spans[b]] = jnp.where(position < live[b], unit, unit[0:1]).astype(jnp.bfloat16)
        writes[b].start()
    for copy in writes:
        copy.wait()


def normalize(embeddings, cluster, live):
    blocks, count, width = embeddings.shape
    return pl.pallas_call(
        unit_kernel,
        out_shape=jax.ShapeDtypeStruct((blocks * count + TAIL, width), jnp.bfloat16),
        in_specs=[anywhere()] * 3,
        out_specs=anywhere(),
        scratch_shapes=[
            pltpu.VMEM(embeddings.shape, jnp.bfloat16),
            pltpu.VMEM((blocks * count + TAIL, width), jnp.bfloat16),
            pltpu.SMEM((blocks,), jnp.int32),
            pltpu.SMEM((blocks,), jnp.int32),
            pltpu.SemaphoreType.DMA((2,)),
            pltpu.SemaphoreType.DMA((blocks,)),
            pltpu.SemaphoreType.DMA((blocks + 1,)),
        ],
        compiler_params=pltpu.CompilerParams(vmem_limit_bytes=VMEM),
        cost_estimate=pl.CostEstimate(flops=4 * embeddings.size, bytes_accessed=4 * embeddings.size, transcendentals=0),
    )(cluster, live, embeddings)


def own_kernel(cluster, live, units, best):
    blocks, count = best.shape
    rows = lax.broadcasted_iota(jnp.int32, (count, count), 0)
    columns = lax.broadcasted_iota(jnp.int32, (count, count), 1)
    other = units[:blocks * count]

    def chunk(i, carry):
        similar = lax.dot_general(
            units[pl.ds(pl.multiple_of(2 * i * count, 2 * count), 2 * count)], other,
            (((1,), (1,)), ((), ())), preferred_element_type=jnp.float32,
        )
        for k in range(2):
            a = 2 * i + k
            top = None
            for j in range(blocks):
                part = similar[k * count:(k + 1) * count, j * count:(j + 1) * count]
                part = part + jnp.where(cluster[a] == cluster[j], 0.0, LOW)
                hidden = (a == j) & ((rows == columns) | (columns >= live[j]))
                part = jnp.where(hidden, LOW, part)
                top = part if top is None else jnp.maximum(top, part)
            best[pl.ds(a, 1)] = jnp.max(top.T, axis=0, keepdims=True)
        return carry

    lax.fori_loop(0, blocks // 2, chunk, 0)


def own_tile(units, cluster, live):
    blocks, count, width = BLOCKS, COUNT, units.shape[1]
    return pl.pallas_call(
        own_kernel,
        out_shape=jax.ShapeDtypeStruct((blocks, count), jnp.float32),
        in_specs=[smem(), smem(), vmem()],
        out_specs=vmem(),
        compiler_params=pltpu.CompilerParams(vmem_limit_bytes=VMEM),
        cost_estimate=pl.CostEstimate(
            flops=2 * (blocks * count) ** 2 * width, bytes_accessed=2 * blocks * count * width, transcendentals=0
        ),
    )(cluster, live, units)


def pairs_kernel(parts, count_jobs, items, begun, jobs, flags, *refs):
    many, count = len(parts), COUNT
    arrays, refs = refs[:many], refs[many:]
    starts, refs = refs[:len(begun)], refs[len(begun):]
    outs, refs = refs[:len(items)], refs[len(items):]
    held, best, tails, listed, ids, arrived, came, moved, state, rows_best = refs
    ends = [
        pltpu.make_async_copy(arrays[i].at[pl.ds(BLOCKS * count, TAIL), pl.ds(0, 128)], tails.at[i], came.at[i])
        for i in range(many)
    ]
    for end in ends:
        end.start()
    for k, item in enumerate(items):
        if item in begun:
            best[k] = starts[begun.index(item)][...]
        else:
            best[k] = jnp.full(best.shape[1:], LOW, jnp.float32)
    for i, end in enumerate(ends):
        end.wait()
        digits = tails[i].astype(jnp.float32)
        listed[i:i + 1] = (digits[0:1] * DIGIT + digits[1:2]).astype(jnp.int32)
    move = pltpu.make_async_copy(listed, ids, moved.at[0])
    move.start()
    move.wait()
    for i in range(many):
        state[i] = 0

    def wanted(j):
        first, second = jobs[5 * j], jobs[5 * j + 1]
        meet = (ids[first, BLOCKS - 1] >= ids[second, 0]) & (ids[first, 0] <= ids[second, BLOCKS - 1])
        return meet & (flags[jobs[5 * j + 2]] > 0)

    def mark(j, carry):
        @pl.when(wanted(j))
        def _():
            state[jobs[5 * j]] = 1
            state[jobs[5 * j + 1]] = 1

        return carry

    lax.fori_loop(0, count_jobs, mark, 0)
    for i in range(many):
        copy = pltpu.make_async_copy(arrays[i].at[pl.ds(0, BLOCKS * count)], held.at[i], arrived.at[i])
        pl.when(state[i] > 0)(copy.start)

    def fetched(i):
        @pl.when(state[i] == 1)
        def _():
            pltpu.make_async_copy(arrays[0].at[pl.ds(0, BLOCKS * count)], held.at[i], arrived.at[i]).wait()
            state[i] = 2

    def tile(first, second, a_out, b_out):
        a, b = held.at[first], held.at[second]
        same = (ids[first, 0] == ids[first, BLOCKS - 1]) & (ids[second, 0] == ids[second, BLOCKS - 1])
        same = same & (ids[first, 0] == ids[second, 0])

        @pl.when(same)
        def _():
            columns = [None] * BLOCKS
            for i in range(BLOCKS // 2):
                similar = lax.dot_general(
                    a[2 * i * count:2 * (i + 1) * count], b[...],
                    (((1,), (1,)), ((), ())), preferred_element_type=jnp.float32,
                )
                for k in range(2):
                    top = None
                    for j in range(BLOCKS):
                        part = similar[k * count:(k + 1) * count, j * count:(j + 1) * count]
                        top = part if top is None else jnp.maximum(top, part)
                        part = jnp.max(part.reshape(count // 8, 8, count), axis=0)
                        columns[j] = part if columns[j] is None else jnp.maximum(columns[j], part)
                    here = slice(2 * i + k, 2 * i + k + 1)
                    top = jnp.max(top.T, axis=0, keepdims=True)
                    best[a_out, here] = jnp.maximum(best[a_out, here], top)
            for j in range(BLOCKS):
                here = slice(j, j + 1)
                top = jnp.max(columns[j], axis=0, keepdims=True)
                best[b_out, here] = jnp.maximum(best[b_out, here], top)

        @pl.when(jnp.logical_not(same))
        def _():
            rows_best[...] = jnp.full(rows_best.shape, LOW, jnp.float32)

            def chunk(n, carry):
                i, j = lax.div(n, BLOCKS // 2), lax.rem(n, BLOCKS // 2)
                meet = ids[first, 2 * i + 1] >= ids[second, 2 * j]

                @pl.when(meet & (ids[first, 2 * i] <= ids[second, 2 * j + 1]))
                def _():
                    similar = lax.dot_general(
                        a[pl.ds(pl.multiple_of(2 * i * count, 2 * count), 2 * count)],
                        b[pl.ds(pl.multiple_of(2 * j * count, 2 * count), 2 * count)],
                        (((1,), (1,)), ((), ())), preferred_element_type=jnp.float32,
                    )
                    columns = [None, None]
                    for k in range(2):
                        here = pl.ds(pl.multiple_of((2 * i + k) * count, count), count)
                        top = rows_best[here]
                        for m in range(2):
                            part = similar[k * count:(k + 1) * count, m * count:(m + 1) * count]
                            part = part + jnp.where(ids[first, 2 * i + k] == ids[second, 2 * j + m], 0.0, LOW)
                            top = jnp.maximum(top, part)
                            columns[m] = part if columns[m] is None else jnp.maximum(columns[m], part)
                        rows_best[here] = top
                    for m in range(2):
                        here = pl.ds(2 * j + m, 1)
                        top = jnp.max(columns[m], axis=0, keepdims=True)
                        best[b_out, here] = jnp.maximum(best[b_out, here], top)

                return carry

            lax.fori_loop(0, (BLOCKS // 2) ** 2, chunk, 0)
            for j in range(BLOCKS):
                top = jnp.max(rows_best[j * count:(j + 1) * count].T, axis=0, keepdims=True)
                best[a_out, j:j + 1] = jnp.maximum(best[a_out, j:j + 1], top)

    def job(j, carry):
        @pl.when(wanted(j))
        def _():
            first, second = jobs[5 * j], jobs[5 * j + 1]
            fetched(first)
            fetched(second)
            tile(first, second, jobs[5 * j + 3], jobs[5 * j + 4])

        return carry

    lax.fori_loop(0, count_jobs, job, 0)
    for k, out in enumerate(outs):
        out[...] = best[k]


def compare(flags, parts, jobs, begun):
    items = []
    for _, item in parts:
        if item not in items:
            items.append(item)
    known = [item for item in items if item in begun]
    arrays = [part[0] for part in parts]
    many, width = len(arrays), arrays[0].shape[1]
    listed = jnp.array(
        [v for f, s, flag in jobs for v in (f, s, flag, items.index(parts[f][1]), items.index(parts[s][1]))], jnp.int32
    )
    found = pl.pallas_call(
        functools.partial(pairs_kernel, [part[1] for part in parts], len(jobs), items, known),
        out_shape=[jax.ShapeDtypeStruct((BLOCKS, COUNT), jnp.float32) for _ in items],
        in_specs=[smem(), smem()] + [anywhere() for _ in arrays] + [vmem() for _ in known],
        out_specs=[vmem() for _ in items],
        scratch_shapes=[
            pltpu.VMEM((many, BLOCKS * COUNT, width), jnp.bfloat16),
            pltpu.VMEM((len(items), BLOCKS, COUNT), jnp.float32),
            pltpu.VMEM((many, TAIL, 128), jnp.bfloat16),
            pltpu.VMEM((8, 128), jnp.int32),
            pltpu.SMEM((8, 128), jnp.int32),
            pltpu.SemaphoreType.DMA((many,)),
            pltpu.SemaphoreType.DMA((many,)),
            pltpu.SemaphoreType.DMA((1,)),
            pltpu.SMEM((many,), jnp.int32),
            pltpu.VMEM((BLOCKS * COUNT, COUNT), jnp.float32),
        ],
        compiler_params=pltpu.CompilerParams(vmem_limit_bytes=VMEM),
        cost_estimate=pl.CostEstimate(
            flops=len(jobs) * 2 * (BLOCKS * COUNT) ** 2 * width,
            bytes_accessed=sum(2 * a.size for a in arrays), transcendentals=0,
        ),
    )(listed, flags, *arrays, *[begun[item] for item in known])
    return {**begun, **dict(zip(items, found))}


def corner_kernel(flags, down, up, out, held, arrive, leave):
    spans = [pl.ds(b * COUNT, COUNT) for b in range(BLOCKS)] + [pl.ds(BLOCKS * COUNT, TAIL)]
    reads = [pltpu.make_async_copy(up.at[span], held.at[span], arrive.at[i]) for i, span in enumerate(spans)]
    writes = [pltpu.make_async_copy(held.at[span], out.at[span], leave.at[i]) for i, span in enumerate(spans)]

    @pl.when(flags[0] > 0)
    def _():
        for read in reads:
            read.start()
        for read, write in zip(reads, writes):
            read.wait()
            write.start()
        for write in writes:
            write.wait()


def with_corner(last, down, up):
    return pl.pallas_call(
        corner_kernel,
        out_shape=jax.ShapeDtypeStruct(down.shape, down.dtype),
        in_specs=[smem(), anywhere(), anywhere()],
        out_specs=anywhere(),
        scratch_shapes=[
            pltpu.VMEM(down.shape, down.dtype),
            pltpu.SemaphoreType.DMA((BLOCKS + 1,)),
            pltpu.SemaphoreType.DMA((BLOCKS + 1,)),
        ],
        input_output_aliases={1: 0},
        compiler_params=pltpu.CompilerParams(vmem_limit_bytes=VMEM),
        cost_estimate=pl.CostEstimate(flops=0, bytes_accessed=4 * down.size, transcendentals=0),
    )(last, down, up)


def ring(devices, by, rows=None):
    return [
        (row * ROW + x, row * ROW + (x + by) % ROW)
        for row in range(devices // ROW) if rows is None or rows(row) for x in range(ROW)
    ]


def column(devices, by, rows=None):
    return [
        (i, i + by * ROW) for i in range(devices)
        if 0 <= i + by * ROW < devices and (rows is None or rows((i + by * ROW) // ROW))
    ]


def body(embeddings, block_cluster, block_rows):
    minor = lax.axis_size(AXES[1])
    devices = lax.axis_size(AXES[0]) * minor
    blocks, count, _ = embeddings.shape
    major = lax.axis_index(AXES[0])
    me = lax.axis_index(AXES).astype(jnp.int32)
    x, row = me % ROW, me // ROW
    last_row = devices // ROW - 1
    even_site = major % 2 == 0

    def even(r):
        return (r * ROW // minor) % 2 == 0

    def odd(r):
        return not even(r)

    right, left = ring(devices, 1), ring(devices, -1)
    below, above = column(devices, 1), column(devices, -1)

    early, late = even_site & (x == 0), ~even_site & (x == ROW - 1)
    between = (x == 1) | (x == 2)
    flags = jnp.stack([
        x >= 0, x < 2, even_site, ~even_site, early, late, even_site & between, ~even_site & between,
        even_site & (x < ROW - 1), ~even_site & (x < ROW - 1),
    ]).astype(jnp.int32)

    units = normalize(embeddings, block_cluster, block_rows)
    up, nxt = shifted(units, below), shifted(units, left)
    down, prv = shifted(units, above), shifted(units, right)
    best = own_tile(units, block_cluster, block_rows)
    up, first_best = lax.optimization_barrier((up, best))
    nxt, second_best = lax.optimization_barrier((nxt, best))
    best = jnp.maximum(first_best, second_best)
    up_next_even = shifted(up, ring(devices, -1, even))
    up_next_odd = shifted(nxt, column(devices, 1, odd))
    down = with_corner((x == ROW - 1).astype(jnp.int32)[None], down, up)
    down_prev_even = shifted(down, [(i, j) for i, j in ring(devices, 1, even) if j % ROW != ROW - 1])
    down_prev_odd = shifted(prv, [(i, j) for i, j in column(devices, -1, odd) if j % ROW in (1, 2)])
    corner_odd = shifted(nxt, [(i, j) for i, j in column(devices, -1, odd) if j % ROW == ROW - 1])

    found = compare(
        flags, [(nxt, "next"), (units, "own"), (prv, "prev"), (up, "up")],
        [(0, 1, ONE), (0, 3, ONE), (0, 2, LEFT_HALF), (1, 3, ONE), (2, 3, ONE)], {},
    )
    found = compare(
        flags, [(prv, "prev"), (down, "down"), (up_next_even, "up_next"), (up_next_odd, "up_next")],
        [(2, 0, EVEN), (2, 1, EVEN_LEFT), (3, 0, ODD), (3, 1, ODD_LEFT)], found,
    )
    found = compare(
        flags,
        [
            (up, "corner"), (down, "down"), (up_next_even, "up_next"), (down_prev_even, "down_prev"),
            (up_next_odd, "up_next"), (down_prev_odd, "down_prev"), (corner_odd, "late"), (down_prev_even, "early"),
        ],
        [(2, 3, EVEN_BETWEEN), (1, 7, EVEN_FIRST), (4, 5, ODD_BETWEEN), (0, 6, ODD_LAST)], found,
    )
    from_prev = shifted(jnp.stack([found["next"], found["up_next"], found["late"]]), right)
    from_next = shifted(jnp.stack([found["prev"], found["early"], found["down_prev"]]), left)
    around = jnp.maximum(from_prev, from_next)
    from_below = shifted(jnp.maximum(jnp.maximum(found["up"], found["corner"]), around[1]), above)
    from_above = shifted(jnp.maximum(found["down"], around[2]), below)
    best = jnp.maximum(jnp.maximum(best, found["own"]), around[0])
    best = jnp.maximum(best, jnp.where(row < last_row, from_below, LOW))
    best = jnp.maximum(best, jnp.where(row > 0, from_above, LOW))
    position = lax.broadcasted_iota(jnp.int32, (blocks, count), 1)
    return jnp.where(position < block_rows[:, None], jnp.maximum(1.0 + best, 0.0) - 1.0, 0.0)


def solution(mesh):
    placed = (P(AXES, None, None), P(AXES), P(AXES))
    return jax.shard_map(body, mesh=mesh, in_specs=placed, out_specs=P(AXES, None), check_vma=False)
```
